32 devices in a mesh: rows: 16 (over z, y, core), pairs: 2 (over x).
Axes of the slice: x: 2, y: 2, z: 4, core: 2. Of those that a mesh axis runs over, the one named last changes fastest.
Arguments:
- loads: float32 [4096, 4096], P('rows', 'pairs'), may hold values from -6 to 6
- col_weights: float32 [4096], P('pairs'), may hold values from 0.3 to 3
- partner_offsets: int32 [2, 2], replicated, may hold values from 0 to 127
- skip_mask: int32 [2, 16], P(None, 'pairs'), may hold values 0 or 1
Outputs:
- rotated: float32 [4096, 4096], P('rows', 'pairs')
- column_power: float32 [4096], P('pairs')
The draws below stay inside these ranges and needn't reach their ends.
All inputs are finite; a program needn't handle non-finite values. No bound on the sum of `skip_mask` on one device may be relied on, other than what follows from the above.
Results may differ from the reference program's by a relative error of at most 0.0003.
Values sent between devices are 32-bit elements; how exact they have to be, the bound alone decides.
A program may use at most 128 MiB of HBM per device.

```python
import math
import jax
import jax.numpy as jnp
from jax import lax

BLOCK = 128
STEPS = 2
INNER = 2
COLS = 4096
PAIRS = 16
PAIRS_DEV = 8
ROWS = 4096
N_PAIRS = 2


def place_ends(array, own_key, least, high):
    shape = array.shape
    spot = [jax.random.randint(jax.random.fold_in(own_key, axis), (), 0, shape[axis]) for axis in range(len(shape))]
    array = array.at[tuple(spot)].set(least)
    longest = shape.index(max(shape))
    spot[longest] = (spot[longest] + 1) % shape[longest]
    return array.at[tuple(spot)].set(high)


def block_scale(key, shape, cuts, smallest, high):
    level, own = 1.0, jax.random.fold_in(key, 6)
    for axis_at, blocks in cuts:
        steps = jnp.exp(jax.random.uniform(jax.random.fold_in(own, axis_at), (blocks,), jnp.float32, smallest / len(cuts), high / len(cuts)))
        level = level * jnp.repeat(steps, shape[axis_at] // blocks).reshape([-1 if axis == axis_at else 1 for axis in range(len(shape))])
    return level


def bell_draw(stream_key, extent, spread, reach, shards=(), held_as=jnp.bfloat16):
    entries = spread * jax.random.normal(stream_key, extent, jnp.float32)
    if shards:
        entries = entries * block_scale(stream_key, extent, shards, -0.22, 0.18)
    return jnp.clip(entries, -reach, reach).astype(held_as)


def setup_inputs(seed: int = 0) -> dict:
    key_list = jax.random.split(jax.random.key(seed), 5)
    loads = bell_draw(key_list[0], (ROWS, COLS), 1.0, 6.0, ((0, 16), (1, 2)), jnp.float32)
    col_weights = jnp.clip(jnp.exp(math.log(3.0) - 2.3025851 * jax.random.uniform(key_list[1], (COLS,), jnp.float32) ** block_scale(key_list[1], (COLS,), ((0, 2),), -0.2, 0.2)), 0.3, 3.0)
    partner_offsets = place_ends(jax.random.randint(key_list[2], (STEPS, INNER), 0, BLOCK), jax.random.fold_in(key_list[2], 1), 0, BLOCK - 1).astype(jnp.int32)
    skip_mask = place_ends((jax.random.randint(key_list[3], (STEPS, PAIRS), 0, 4) < 1).astype(jnp.int32), jax.random.fold_in(key_list[3], 1), 0, 1)
    return {"loads": loads, "col_weights": col_weights, "partner_offsets": partner_offsets, "skip_mask": skip_mask}


precise = lax.Precision.HIGHEST

def turn_columns(matrix, cosine_values, sine_values, offset):
    half_width = matrix.shape[-1] // 2
    left_part = matrix[..., :half_width]
    right_part = jnp.roll(matrix[..., half_width:], -offset, axis=-1)
    cosine_grid = cosine_values[:, None, :]
    sine_grid = sine_values[:, None, :]
    new_left = cosine_grid * left_part - sine_grid * right_part
    new_right = jnp.roll(sine_grid * left_part + cosine_grid * right_part, offset, axis=-1)
    return jnp.concatenate([new_left, new_right], axis=-1)

def rotate_pair(gram_matrix, offsets_step, skip_step):
    half_width = gram_matrix.shape[-1] // 2
    identity = jnp.broadcast_to(jnp.eye(2 * half_width, dtype=jnp.float32), gram_matrix.shape)
    turned = gram_matrix
    rotation = identity
    for step_round in range(offsets_step.shape[0]):
        offset = offsets_step[step_round]
        diagonal_values = jnp.diagonal(turned, axis1=1, axis2=2)
        first_norms = diagonal_values[:, :half_width]
        second_norms = jnp.roll(diagonal_values[:, half_width:], -offset, axis=1)
        coupling = jnp.diagonal(jnp.roll(turned[:, :half_width, half_width:], -offset, axis=2), axis1=1, axis2=2)
        half_gap = 0.5 * (second_norms - first_norms)
        gap_sign = jnp.where(half_gap >= 0.0, 1.0, -1.0)
        denominator = jnp.maximum(jnp.abs(half_gap) + jnp.sqrt(half_gap * half_gap + coupling * coupling), 1e-06 * (first_norms + second_norms))
        tangent = gap_sign * coupling / denominator
        cosine_values = 1.0 / jnp.sqrt(1.0 + tangent * tangent)
        sine_values = tangent * cosine_values
        turned = turn_columns(turned, cosine_values, sine_values, offset)
        turned = jnp.swapaxes(turn_columns(jnp.swapaxes(turned, 1, 2), cosine_values, sine_values, offset), 1, 2)
        rotation = turn_columns(rotation, cosine_values, sine_values, offset)
    unskipped = (skip_step == 0)[:, None, None]
    return (jnp.where(unskipped, rotation, identity), jnp.where(unskipped, turned, gram_matrix))

def reference(loads, col_weights, partner_offsets, skip_mask):
    weighted = loads * col_weights[None, :]
    blocks = weighted.reshape(ROWS, N_PAIRS, 2, PAIRS_DEV, BLOCK).transpose(2, 1, 3, 0, 4).reshape(2, PAIRS, ROWS, BLOCK)
    upper_blocks = blocks[0]
    lower_blocks = blocks[1]
    for step_index in range(STEPS):
        joined = jnp.concatenate([upper_blocks, lower_blocks], axis=-1)
        gram_matrix = jnp.einsum('prc,prd->pcd', joined, joined, precision=precise, preferred_element_type=jnp.float32)
        rotation, turned = rotate_pair(gram_matrix, partner_offsets[step_index], skip_mask[step_index])
        joined = jnp.einsum('prc,pcd->prd', joined, rotation, precision=precise, preferred_element_type=jnp.float32)
        upper_blocks = joined[..., :BLOCK]
        lower_blocks = joined[..., BLOCK:]
        if step_index + 1 < STEPS:
            new_upper = jnp.concatenate([upper_blocks[:1], lower_blocks[:1], upper_blocks[1:-1]], axis=0)
            new_lower = jnp.concatenate([lower_blocks[1:], upper_blocks[-1:]], axis=0)
            upper_blocks = new_upper
            lower_blocks = new_lower
    final_blocks = jnp.stack([upper_blocks, lower_blocks]).reshape(2, N_PAIRS, PAIRS_DEV, ROWS, BLOCK)
    rotated = final_blocks.transpose(3, 1, 0, 2, 4).reshape(ROWS, COLS)
    column_power = lax.optimization_barrier(jnp.sum(rotated * rotated, axis=0)) / ROWS
    return (rotated, column_power)
```

```python
import functools
import jax
import jax.numpy as jnp
from jax import lax
from jax.experimental import pallas as pl
from jax.experimental.pallas import tpu as pltpu
from jax.sharding import PartitionSpec as P

BLOCK = 128
STEPS = 2
TILE = 8
CHUNK = 64
MESH = pl.DeviceIdType.MESH


def rolled(x, shift):
    return pltpu.roll(x, shift, 1)


def fold(x):
    return jnp.sum(x.reshape(x.shape[0] // TILE, TILE, BLOCK), axis=0)


def shifts_of(offsets, step):
    first, second = offsets[step, 0], offsets[step, 1]
    to_first = lax.rem(BLOCK - first, BLOCK)
    to_second = lax.rem(BLOCK - second, BLOCK)
    between = lax.rem(BLOCK + first - second, BLOCK)
    return to_first, to_second, between, second


def products(upper, lower, shifts, rows, weights, partial):
    to_first, to_second, between, _ = shifts

    def body(at, sums):
        spot = pl.ds(pl.multiple_of(at * CHUNK, CHUNK), CHUNK)
        u, l = upper[spot, :], lower[spot, :]
        if weights is not None:
            u, l = u * weights[0], l * weights[1]
            upper[spot, :] = u
            lower[spot, :] = l
        lp, ud, ld = rolled(l, to_first), rolled(u, between), rolled(l, to_second)
        pairs = ((u, u), (lp, lp), (u, lp), (u, ud), (u, ld), (lp, ud), (lp, ld))
        return tuple(total + fold(a * b) for total, (a, b) in zip(sums, pairs))

    zero = jnp.zeros((TILE, BLOCK), jnp.float32)
    sums = lax.fori_loop(0, rows // CHUNK, body, (zero,) * 7)
    for at, total in enumerate(sums):
        partial[pl.ds(at, 1), :] = jnp.sum(total, axis=0, keepdims=True)
    partial[pl.ds(7, 1), :] = jnp.zeros((1, BLOCK), jnp.float32)


def angle(a, b, g):
    half_gap = 0.5 * (b - a)
    sign = jnp.where(half_gap >= 0.0, 1.0, -1.0)
    denominator = jnp.maximum(
        jnp.abs(half_gap) + jnp.sqrt(half_gap * half_gap + g * g), 1e-06 * (a + b)
    )
    t = sign * g / denominator
    c = 1.0 / jnp.sqrt(1.0 + t * t)
    return c, t * c


def norms(a, b, g, c, s):
    cross = 2.0 * c * s * g
    return c * c * a - cross + s * s * b, s * s * a + cross + c * c * b


def turn(total, skip, shifts):
    _, _, between, back = shifts
    row = [jnp.broadcast_to(total[at : at + 1, :], (TILE, BLOCK)) for at in range(7)]
    a, b, g, u_ud, u_ld, l_ud, l_ld = row
    keep = jnp.full((TILE, BLOCK), skip, jnp.int32) == 0
    c, s = angle(a, b, g)
    c, s = jnp.where(keep, c, 1.0), jnp.where(keep, s, 0.0)
    a1, b1 = norms(a, b, g, c, s)
    cd, sd, bd = rolled(c, between), rolled(s, between), rolled(b1, between)
    g1 = c * (sd * u_ud + cd * u_ld) - s * (sd * l_ud + cd * l_ld)
    c2, s2 = angle(a1, bd, g1)
    c2, s2 = jnp.where(keep, c2, 1.0), jnp.where(keep, s2, 0.0)
    a2, b2 = norms(a1, bd, g1, c2, s2)
    place = lax.broadcasted_iota(jnp.int32, (TILE, BLOCK), 0)
    tile = rolled(b2, back)
    for at, value in enumerate((c, s, cd, sd, c2, s2, a2)):
        tile = jnp.where(place == at, value, tile)
    return tile


def rotate(upper, lower, new_upper, new_lower, coefs, shifts, rows):
    to_first, to_second, between, back = shifts
    tile = coefs[...]
    c, s, cd, sd, c2, s2 = (tile[at : at + 1, :] for at in range(6))
    up = (c2 * c, -c2 * s, -s2 * sd, -s2 * cd)
    low = (s2 * c, -s2 * s, c2 * sd, c2 * cd)

    def body(at, carry):
        spot = pl.ds(pl.multiple_of(at * CHUNK, CHUNK), CHUNK)
        u, l = upper[spot, :], lower[spot, :]
        parts = (u, rolled(l, to_first), rolled(u, between), rolled(l, to_second))
        new_upper[spot, :] = sum(f * x for f, x in zip(up, parts))
        new_lower[spot, :] = rolled(sum(f * x for f, x in zip(low, parts)), back)
        return carry

    lax.fori_loop(0, rows // CHUNK, body, 0)


def kernel(
    n, n_pairs, half, rows,
    loads, weights, offsets, skips,
    rotated, power,
    data, moved, partial, arrived, coefs,
    load_sem, store_sem, sum_sem, pair_sem,
):
    me, position = lax.axis_index("rows"), lax.axis_index("pairs")
    copies = n // half
    own, group = me // copies, lax.rem(me, copies)
    not_first = (position + n_pairs - 1) // n_pairs
    is_last = (position + 1) // n_pairs

    def load(block):
        columns = pl.ds(pl.multiple_of(block * BLOCK, BLOCK), BLOCK)
        return pltpu.make_async_copy(loads.at[:, columns], data.at[block], load_sem.at[block])

    def store(block):
        columns = pl.ds(pl.multiple_of(block * BLOCK, BLOCK), BLOCK)
        return pltpu.make_async_copy(data.at[block], rotated.at[:, columns], store_sem.at[block])

    for k in range(half):
        load(k).start()
        load(half + k).start()

    barrier = pltpu.get_barrier_semaphore()

    @pl.loop(1, n)
    def _(by):
        pl.semaphore_signal(
            barrier, inc=1, device_id={"rows": lax.rem(me + by, n)}, device_id_type=MESH
        )

    @pl.when(position > 0)
    def _():
        pl.semaphore_signal(
            barrier, inc=1, device_id={"pairs": position - 1}, device_id_type=MESH
        )

    @pl.when(position < n_pairs - 1)
    def _():
        pl.semaphore_signal(
            barrier, inc=1, device_id={"pairs": position + 1}, device_id_type=MESH
        )

    def all_coefs(step, shifts):
        def give(by):
            to = lax.rem(me + by, n)
            return pltpu.make_async_remote_copy(
                src_ref=partial.at[step, to // copies],
                dst_ref=arrived.at[step, me],
                send_sem=sum_sem.at[step, 0],
                recv_sem=sum_sem.at[step, 1],
                device_id={"rows": to},
                device_id_type=MESH,
            )

        def spread(by):
            to = lax.rem(own + by, half) * copies + group
            return pltpu.make_async_remote_copy(
                src_ref=coefs.at[step, own],
                dst_ref=coefs.at[step, own],
                send_sem=sum_sem.at[step, 2],
                recv_sem=sum_sem.at[step, 3],
                device_id={"rows": to},
                device_id_type=MESH,
            )

        @pl.loop(1, n)
        def _(by):
            give(by).start()

        arrived[step, me] = partial[step, own]
        some = arrived.at[step, pl.ds(0, n - 1)]
        pltpu.make_async_copy(some, some, sum_sem.at[step, 1]).wait()
        total = jnp.sum(arrived[step], axis=0)
        coefs[step, own] = turn(total, skips[step, own], shifts)

        @pl.loop(1, half)
        def _(by):
            spread(by).start()

        rest = coefs.at[step, pl.ds(0, half - 1)]
        pltpu.make_async_copy(rest, rest, sum_sem.at[step, 3]).wait()
        pltpu.make_async_copy(some, some, sum_sem.at[step, 0]).wait()
        pltpu.make_async_copy(rest, rest, sum_sem.at[step, 2]).wait()

    shifts = shifts_of(offsets, 0)

    @pl.loop(0, half)
    def _(k):
        load(k).wait()
        load(half + k).wait()
        scale = (weights[pl.ds(k, 1), :], weights[pl.ds(half + k, 1), :])
        products(data.at[k], data.at[half + k], shifts, rows, scale, partial.at[0, k])

    pl.semaphore_wait(barrier, n - 1 + not_first + 1 - is_last)
    all_coefs(0, shifts)

    def first_turn(k, upper_to, lower_to):
        rotate(
            data.at[k], data.at[half + k], moved.at[upper_to], moved.at[lower_to],
            coefs.at[0, k], shifts, rows,
        )

    out_low, out_up = 2 * half, 2 * half + 1
    low_zero = (1 - not_first) + out_low * not_first
    up_last = (2 * half - 1) * is_last + out_up * (1 - is_last)
    up_copy = pltpu.make_async_remote_copy(
        src_ref=moved.at[out_up],
        dst_ref=moved.at[0],
        send_sem=pair_sem.at[0],
        recv_sem=pair_sem.at[1],
        device_id={"pairs": lax.rem(position + 1, n_pairs)},
        device_id_type=MESH,
    )
    low_copy = pltpu.make_async_remote_copy(
        src_ref=moved.at[out_low],
        dst_ref=moved.at[2 * half - 1],
        send_sem=pair_sem.at[2],
        recv_sem=pair_sem.at[3],
        device_id={"pairs": lax.rem(position + n_pairs - 1, n_pairs)},
        device_id_type=MESH,
    )

    first_turn(half - 1, up_last, 2 * half - 2)

    @pl.when(position < n_pairs - 1)
    def _():
        up_copy.start()

    first_turn(0, not_first, low_zero)

    @pl.when(position > 0)
    def _():
        low_copy.start()

    @pl.loop(1, half - 1)
    def _(k):
        first_turn(k, k + 1, half + k - 1)

    later = shifts_of(offsets, 1)

    def second_products(k):
        products(moved.at[k], moved.at[half + k], later, rows, None, partial.at[1, k])

    @pl.loop(1, half - 1)
    def _(k):
        second_products(k)

    @pl.when(position > 0)
    def _():
        up_copy.wait_recv()
        low_copy.wait_send()

    @pl.when(position < n_pairs - 1)
    def _():
        low_copy.wait_recv()
        up_copy.wait_send()

    second_products(0)
    second_products(half - 1)
    all_coefs(1, later)

    @pl.loop(0, half)
    def _(k):
        rotate(
            moved.at[k], moved.at[half + k], data.at[k], data.at[half + k],
            coefs.at[1, k], later, rows,
        )
        store(k).start()
        store(half + k).start()
        tile = coefs[1, k] * (1.0 / (rows * n))
        power[pl.ds(k, 1), :] = tile[6:7, :]
        power[pl.ds(half + k, 1), :] = tile[7:8, :]

    @pl.loop(0, 2 * half)
    def _(block):
        store(block).wait()


def per_device(n, n_pairs, loads, col_weights, partner_offsets, skip_mask):
    rows, columns = loads.shape
    half = columns // (2 * BLOCK)
    tiles = (TILE, BLOCK)
    rotated, power = pl.pallas_call(
        functools.partial(kernel, n, n_pairs, half, rows),
        out_shape=(
            jax.ShapeDtypeStruct(loads.shape, jnp.float32),
            jax.ShapeDtypeStruct((2 * half, BLOCK), jnp.float32),
        ),
        in_specs=[
            pl.BlockSpec(memory_space=pl.ANY),
            pl.BlockSpec(memory_space=pltpu.VMEM),
            pl.BlockSpec(memory_space=pltpu.SMEM),
            pl.BlockSpec(memory_space=pltpu.SMEM),
        ],
        out_specs=(
            pl.BlockSpec(memory_space=pl.ANY),
            pl.BlockSpec(memory_space=pltpu.VMEM),
        ),
        scratch_shapes=[
            pltpu.VMEM((2 * half, rows, BLOCK), jnp.float32),
            pltpu.VMEM((2 * half + 2, rows, BLOCK), jnp.float32),
            pltpu.VMEM((STEPS, half) + tiles, jnp.float32),
            pltpu.VMEM((STEPS, n) + tiles, jnp.float32),
            pltpu.VMEM((STEPS, half) + tiles, jnp.float32),
            pltpu.SemaphoreType.DMA((2 * half,)),
            pltpu.SemaphoreType.DMA((2 * half,)),
            pltpu.SemaphoreType.DMA((STEPS, 4)),
            pltpu.SemaphoreType.DMA((4,)),
        ],
        compiler_params=pltpu.CompilerParams(
            collective_id=0, has_side_effects=True, vmem_limit_bytes=16 * 1024 * 1024
        ),
        cost_estimate=pl.CostEstimate(
            flops=60 * loads.size, bytes_accessed=8 * loads.size, transcendentals=0
        ),
    )(loads, col_weights.reshape(2 * half, BLOCK), partner_offsets, skip_mask)
    return rotated, power.reshape(columns)


def solution(mesh):
    in_specs = (P("rows", "pairs"), P("pairs"), P(), P(None, "pairs"))
    out_specs = (P("rows", "pairs"), P("pairs"))
    return jax.shard_map(
        functools.partial(per_device, mesh.shape["rows"], mesh.shape["pairs"]),
        mesh=mesh, in_specs=in_specs, out_specs=out_specs, check_vma=False,
    )
```

```python
import functools
import jax
import jax.numpy as jnp
from jax import lax
from jax.experimental import pallas as pl
from jax.experimental.pallas import tpu as pltpu
from jax.sharding import PartitionSpec as P

BLOCK = 128
STEPS = 2
TILE = 8
CHUNK = 32
MESH = pl.DeviceIdType.MESH


def rolled(x, shift):
    return pltpu.roll(x, shift, 1)


def fold(x):
    return jnp.sum(x.reshape(x.shape[0] // TILE, TILE, BLOCK), axis=0)


def shifts_of(offsets, step):
    first, second = offsets[step, 0], offsets[step, 1]
    to_first = lax.rem(BLOCK - first, BLOCK)
    to_second = lax.rem(BLOCK - second, BLOCK)
    between = lax.rem(BLOCK + first - second, BLOCK)
    return to_first, to_second, between, second


def products(upper, lower, shifts, rows, weights, partial):
    to_first, to_second, between, _ = shifts

    def body(at, sums):
        spot = pl.ds(pl.multiple_of(at * CHUNK, CHUNK), CHUNK)
        u, l = upper[spot, :], lower[spot, :]
        if weights is not None:
            u, l = u * weights[0], l * weights[1]
            upper[spot, :] = u
            lower[spot, :] = l
        lp, ud, ld = rolled(l, to_first), rolled(u, between), rolled(l, to_second)
        pairs = ((u, u), (lp, lp), (u, lp), (u, ud), (u, ld), (lp, ud), (lp, ld))
        return tuple(total + fold(a * b) for total, (a, b) in zip(sums, pairs))

    zero = jnp.zeros((TILE, BLOCK), jnp.float32)
    sums = lax.fori_loop(0, rows // CHUNK, body, (zero,) * 7, unroll=True)
    for at, total in enumerate(sums):
        partial[pl.ds(at, 1), :] = jnp.sum(total, axis=0, keepdims=True)
    partial[pl.ds(7, 1), :] = jnp.zeros((1, BLOCK), jnp.float32)


def angle(a, b, g):
    half_gap = 0.5 * (b - a)
    sign = jnp.where(half_gap >= 0.0, 1.0, -1.0)
    denominator = jnp.maximum(
        jnp.abs(half_gap) + jnp.sqrt(half_gap * half_gap + g * g), 1e-06 * (a + b)
    )
    t = sign * g / denominator
    c = 1.0 / jnp.sqrt(1.0 + t * t)
    return c, t * c


def norms(a, b, g, c, s):
    cross = 2.0 * c * s * g
    return c * c * a - cross + s * s * b, s * s * a + cross + c * c * b


def turn(total, skip, shifts):
    _, _, between, back = shifts
    row = [jnp.broadcast_to(total[at : at + 1, :], (TILE, BLOCK)) for at in range(7)]
    a, b, g, u_ud, u_ld, l_ud, l_ld = row
    keep = jnp.full((TILE, BLOCK), skip, jnp.int32) == 0
    c, s = angle(a, b, g)
    c, s = jnp.where(keep, c, 1.0), jnp.where(keep, s, 0.0)
    a1, b1 = norms(a, b, g, c, s)
    cd, sd, bd = rolled(c, between), rolled(s, between), rolled(b1, between)
    g1 = c * (sd * u_ud + cd * u_ld) - s * (sd * l_ud + cd * l_ld)
    c2, s2 = angle(a1, bd, g1)
    c2, s2 = jnp.where(keep, c2, 1.0), jnp.where(keep, s2, 0.0)
    a2, b2 = norms(a1, bd, g1, c2, s2)
    place = lax.broadcasted_iota(jnp.int32, (TILE, BLOCK), 0)
    tile = rolled(b2, back)
    for at, value in enumerate((c, s, cd, sd, c2, s2, a2)):
        tile = jnp.where(place == at, value, tile)
    return tile


def rotate(upper, lower, new_upper, new_lower, coefs, shifts, rows):
    to_first, to_second, between, back = shifts
    tile = coefs[...]
    c, s, cd, sd, c2, s2 = (tile[at : at + 1, :] for at in range(6))
    up = (c2 * c, -c2 * s, -s2 * sd, -s2 * cd)
    low = (s2 * c, -s2 * s, c2 * sd, c2 * cd)

    def body(at, carry):
        spot = pl.ds(pl.multiple_of(at * CHUNK, CHUNK), CHUNK)
        u, l = upper[spot, :], lower[spot, :]
        parts = (u, rolled(l, to_first), rolled(u, between), rolled(l, to_second))
        new_upper[spot, :] = sum(f * x for f, x in zip(up, parts))
        new_lower[spot, :] = rolled(sum(f * x for f, x in zip(low, parts)), back)
        return carry

    lax.fori_loop(0, rows // CHUNK, body, 0, unroll=True)


def kernel(
    n, n_pairs, half, rows,
    loads, weights_in, offsets_in, skips_in,
    rotated, power,
    weights, offsets, skips, small_sem, data, moved, partial, arrived, coefs,
    load_sem, store_sem, sum_sem, pair_sem,
):
    me, position = lax.axis_index("rows"), lax.axis_index("pairs")
    copies = n // half
    own, group = me // copies, lax.rem(me, copies)
    not_first = (position + n_pairs - 1) // n_pairs
    is_last = (position + 1) // n_pairs

    def load(block):
        columns = pl.ds(pl.multiple_of(block * BLOCK, BLOCK), BLOCK)
        return pltpu.make_async_copy(loads.at[:, columns], data.at[block], load_sem.at[block])

    def store(block):
        columns = pl.ds(pl.multiple_of(block * BLOCK, BLOCK), BLOCK)
        return pltpu.make_async_copy(data.at[block], rotated.at[:, columns], store_sem.at[block])

    small = [
        pltpu.make_async_copy(offsets_in, offsets, small_sem.at[0]),
        pltpu.make_async_copy(weights_in, weights, small_sem.at[1]),
        pltpu.make_async_copy(skips_in, skips, small_sem.at[2]),
    ]
    for copy in small:
        copy.start()
    for k in range(half):
        load(k).start()
        load(half + k).start()

    barrier = pltpu.get_barrier_semaphore()

    @pl.loop(1, n)
    def _(by):
        pl.semaphore_signal(
            barrier, inc=1, device_id={"rows": lax.rem(me + by, n)}, device_id_type=MESH
        )

    @pl.when(position > 0)
    def _():
        pl.semaphore_signal(
            barrier, inc=1, device_id={"pairs": position - 1}, device_id_type=MESH
        )

    @pl.when(position < n_pairs - 1)
    def _():
        pl.semaphore_signal(
            barrier, inc=1, device_id={"pairs": position + 1}, device_id_type=MESH
        )

    def all_coefs(step, shifts):
        def give(by):
            to = lax.rem(me + by, n)
            return pltpu.make_async_remote_copy(
                src_ref=partial.at[step, to // copies],
                dst_ref=arrived.at[step, me],
                send_sem=sum_sem.at[step, 0],
                recv_sem=sum_sem.at[step, 1],
                device_id={"rows": to},
                device_id_type=MESH,
            )

        def spread(by):
            to = lax.rem(own + by, half) * copies + group
            return pltpu.make_async_remote_copy(
                src_ref=coefs.at[step, own],
                dst_ref=coefs.at[step, own],
                send_sem=sum_sem.at[step, 2],
                recv_sem=sum_sem.at[step, 3],
                device_id={"rows": to},
                device_id_type=MESH,
            )

        @pl.loop(1, n)
        def _(by):
            give(by).start()

        arrived[step, me] = partial[step, own]
        some = arrived.at[step, pl.ds(0, n - 1)]
        pltpu.make_async_copy(some, some, sum_sem.at[step, 1]).wait()
        total = jnp.sum(arrived[step], axis=0)
        coefs[step, own] = turn(total, skips[step, own], shifts)

        @pl.loop(1, half)
        def _(by):
            spread(by).start()

        rest = coefs.at[step, pl.ds(0, half - 1)]
        pltpu.make_async_copy(rest, rest, sum_sem.at[step, 3]).wait()
        pltpu.make_async_copy(some, some, sum_sem.at[step, 0]).wait()
        pltpu.make_async_copy(rest, rest, sum_sem.at[step, 2]).wait()

    for copy in small:
        copy.wait()
    shifts = shifts_of(offsets, 0)

    @pl.loop(0, half)
    def _(k):
        load(k).wait()
        load(half + k).wait()
        scale = (weights[pl.ds(k, 1), :], weights[pl.ds(half + k, 1), :])
        products(data.at[k], data.at[half + k], shifts, rows, scale, partial.at[0, k])

    pl.semaphore_wait(barrier, n - 1 + not_first + 1 - is_last)
    all_coefs(0, shifts)

    def first_turn(k, upper_to, lower_to):
        rotate(
            data.at[k], data.at[half + k], moved.at[upper_to], moved.at[lower_to],
            coefs.at[0, k], shifts, rows,
        )

    out_low, out_up = 2 * half, 2 * half + 1
    low_zero = (1 - not_first) + out_low * not_first
    up_last = (2 * half - 1) * is_last + out_up * (1 - is_last)
    up_copy = pltpu.make_async_remote_copy(
        src_ref=moved.at[out_up],
        dst_ref=moved.at[0],
        send_sem=pair_sem.at[0],
        recv_sem=pair_sem.at[1],
        device_id={"pairs": lax.rem(position + 1, n_pairs)},
        device_id_type=MESH,
    )
    low_copy = pltpu.make_async_remote_copy(
        src_ref=moved.at[out_low],
        dst_ref=moved.at[2 * half - 1],
        send_sem=pair_sem.at[2],
        recv_sem=pair_sem.at[3],
        device_id={"pairs": lax.rem(position + n_pairs - 1, n_pairs)},
        device_id_type=MESH,
    )

    first_turn(half - 1, up_last, 2 * half - 2)

    @pl.when(position < n_pairs - 1)
    def _():
        up_copy.start()

    first_turn(0, not_first, low_zero)

    @pl.when(position > 0)
    def _():
        low_copy.start()

    @pl.loop(1, half - 1)
    def _(k):
        first_turn(k, k + 1, half + k - 1)

    later = shifts_of(offsets, 1)

    def second_products(k):
        products(moved.at[k], moved.at[half + k], later, rows, None, partial.at[1, k])

    @pl.loop(1, half - 1)
    def _(k):
        second_products(k)

    @pl.when(position > 0)
    def _():
        up_copy.wait_recv()
        low_copy.wait_send()

    @pl.when(position < n_pairs - 1)
    def _():
        low_copy.wait_recv()
        up_copy.wait_send()

    second_products(0)
    second_products(half - 1)
    all_coefs(1, later)

    @pl.loop(0, half)
    def _(k):
        rotate(
            moved.at[k], moved.at[half + k], data.at[k], data.at[half + k],
            coefs.at[1, k], later, rows,
        )
        store(k).start()
        store(half + k).start()
        tile = coefs[1, k] * (1.0 / (rows * n))
        power[pl.ds(k, 1), :] = tile[6:7, :]
        power[pl.ds(half + k, 1), :] = tile[7:8, :]

    @pl.loop(0, 2 * half)
    def _(block):
        store(block).wait()


def per_device(n, n_pairs, loads, col_weights, partner_offsets, skip_mask):
    rows, columns = loads.shape
    half = columns // (2 * BLOCK)
    tiles = (TILE, BLOCK)
    rotated, power = pl.pallas_call(
        functools.partial(kernel, n, n_pairs, half, rows),
        out_shape=(
            jax.ShapeDtypeStruct(loads.shape, jnp.float32),
            jax.ShapeDtypeStruct((2 * half, BLOCK), jnp.float32),
        ),
        in_specs=[
            pl.BlockSpec(memory_space=pltpu.HBM),
            pl.BlockSpec(memory_space=pltpu.HBM),
            pl.BlockSpec(memory_space=pltpu.HBM),
            pl.BlockSpec(memory_space=pltpu.HBM),
        ],
        out_specs=(
            pl.BlockSpec(memory_space=pl.ANY),
            pl.BlockSpec(memory_space=pltpu.VMEM),
        ),
        scratch_shapes=[
            pltpu.VMEM((2 * half, BLOCK), jnp.float32),
            pltpu.SMEM(partner_offsets.shape, jnp.int32),
            pltpu.SMEM(skip_mask.shape, jnp.int32),
            pltpu.SemaphoreType.DMA((3,)),
            pltpu.VMEM((2 * half, rows, BLOCK), jnp.float32),
            pltpu.VMEM((2 * half + 2, rows, BLOCK), jnp.float32),
            pltpu.VMEM((STEPS, half) + tiles, jnp.float32),
            pltpu.VMEM((STEPS, n) + tiles, jnp.float32),
            pltpu.VMEM((STEPS, half) + tiles, jnp.float32),
            pltpu.SemaphoreType.DMA((2 * half,)),
            pltpu.SemaphoreType.DMA((2 * half,)),
            pltpu.SemaphoreType.DMA((STEPS, 4)),
            pltpu.SemaphoreType.DMA((4,)),
        ],
        compiler_params=pltpu.CompilerParams(
            collective_id=0, has_side_effects=True, vmem_limit_bytes=60 * 1024 * 1024
        ),
        cost_estimate=pl.CostEstimate(
            flops=60 * loads.size, bytes_accessed=8 * loads.size, transcendentals=0
        ),
    )(loads, col_weights.reshape(2 * half, BLOCK), partner_offsets, skip_mask)
    return rotated, power.reshape(columns)


def solution(mesh):
    in_specs = (P("rows", "pairs"), P("pairs"), P(), P(None, "pairs"))
    out_specs = (P("rows", "pairs"), P("pairs"))
    return jax.shard_map(
        functools.partial(per_device, mesh.shape["rows"], mesh.shape["pairs"]),
        mesh=mesh, in_specs=in_specs, out_specs=out_specs, check_vma=False,
    )
```

```python
import functools
import jax
import jax.numpy as jnp
from jax import lax
from jax.experimental import pallas as pl
from jax.experimental.pallas import tpu as pltpu
from jax.sharding import PartitionSpec as P

BLOCK = 128
STEPS = 2
TILE = 8
CHUNK = 32
MESH = pl.DeviceIdType.MESH


def rolled(x, shift):
    return pltpu.roll(x, shift, 1)


def fold(x):
    return jnp.sum(x.reshape(x.shape[0] // TILE, TILE, BLOCK), axis=0)


def shifts_of(offsets, step):
    first, second = offsets[step, 0], offsets[step, 1]
    to_first = lax.rem(BLOCK - first, BLOCK)
    to_second = lax.rem(BLOCK - second, BLOCK)
    between = lax.rem(BLOCK + first - second, BLOCK)
    return to_first, to_second, between, second


def products(upper, lower, shifts, rows, weights, partial):
    to_first, to_second, between, _ = shifts

    def body(at, sums):
        spot = pl.ds(pl.multiple_of(at * CHUNK, CHUNK), CHUNK)
        u, l = upper[spot, :], lower[spot, :]
        if weights is not None:
            u, l = u * weights[0], l * weights[1]
            upper[spot, :] = u
            lower[spot, :] = l
        lp, ud, ld = rolled(l, to_first), rolled(u, between), rolled(l, to_second)
        pairs = ((u, u), (lp, lp), (u, lp), (u, ud), (u, ld), (lp, ud), (lp, ld))
        return tuple(total + fold(a * b) for total, (a, b) in zip(sums, pairs))

    zero = jnp.zeros((TILE, BLOCK), jnp.float32)
    sums = lax.fori_loop(0, rows // CHUNK, body, (zero,) * 7, unroll=True)
    for at, total in enumerate(sums):
        partial[pl.ds(at, 1), :] = jnp.sum(total, axis=0, keepdims=True)
    partial[pl.ds(7, 1), :] = jnp.zeros((1, BLOCK), jnp.float32)


def angle(a, b, g):
    half_gap = 0.5 * (b - a)
    sign = jnp.where(half_gap >= 0.0, 1.0, -1.0)
    denominator = jnp.maximum(
        jnp.abs(half_gap) + jnp.sqrt(half_gap * half_gap + g * g), 1e-06 * (a + b)
    )
    t = sign * g / denominator
    c = 1.0 / jnp.sqrt(1.0 + t * t)
    return c, t * c


def norms(a, b, g, c, s):
    cross = 2.0 * c * s * g
    return c * c * a - cross + s * s * b, s * s * a + cross + c * c * b


def turn(total, skip, shifts):
    _, _, between, back = shifts
    row = [jnp.broadcast_to(total[at : at + 1, :], (TILE, BLOCK)) for at in range(7)]
    a, b, g, u_ud, u_ld, l_ud, l_ld = row
    keep = jnp.full((TILE, BLOCK), skip, jnp.int32) == 0
    c, s = angle(a, b, g)
    c, s = jnp.where(keep, c, 1.0), jnp.where(keep, s, 0.0)
    a1, b1 = norms(a, b, g, c, s)
    cd, sd, bd = rolled(c, between), rolled(s, between), rolled(b1, between)
    g1 = c * (sd * u_ud + cd * u_ld) - s * (sd * l_ud + cd * l_ld)
    c2, s2 = angle(a1, bd, g1)
    c2, s2 = jnp.where(keep, c2, 1.0), jnp.where(keep, s2, 0.0)
    a2, b2 = norms(a1, bd, g1, c2, s2)
    place = lax.broadcasted_iota(jnp.int32, (TILE, BLOCK), 0)
    tile = rolled(b2, back)
    for at, value in enumerate((c, s, cd, sd, c2, s2, a2)):
        tile = jnp.where(place == at, value, tile)
    return tile


def rotate(upper, lower, new_upper, new_lower, coefs, shifts, rows):
    to_first, to_second, between, back = shifts
    tile = coefs[...]
    c, s, cd, sd, c2, s2 = (tile[at : at + 1, :] for at in range(6))
    up = (c2 * c, -c2 * s, -s2 * sd, -s2 * cd)
    low = (s2 * c, -s2 * s, c2 * sd, c2 * cd)

    def body(at, carry):
        spot = pl.ds(pl.multiple_of(at * CHUNK, CHUNK), CHUNK)
        u, l = upper[spot, :], lower[spot, :]
        parts = (u, rolled(l, to_first), rolled(u, between), rolled(l, to_second))
        new_upper[spot, :] = sum(f * x for f, x in zip(up, parts))
        new_lower[spot, :] = rolled(sum(f * x for f, x in zip(low, parts)), back)
        return carry

    lax.fori_loop(0, rows // CHUNK, body, 0, unroll=True)


def column_block(array, block):
    return array.at[:, pl.ds(pl.multiple_of(block * BLOCK, BLOCK), BLOCK)]


def turning_kernel(
    n, n_pairs, half, rows,
    loads, weights_in, offsets_in, skips_in,
    moved_out, coefs_out,
    weights, offsets, skips, data, moved, partial, arrived, coefs,
    small_sem, load_sem, store_sem, give_sem, arrive_sem, spread_sem, coef_sem, pair_sem,
):
    me, position = lax.axis_index("rows"), lax.axis_index("pairs")
    copies = n // half
    own, group = me // copies, lax.rem(me, copies)
    not_first = (position + n_pairs - 1) // n_pairs
    is_last = (position + 1) // n_pairs

    def load(block):
        return pltpu.make_async_copy(
            column_block(loads, block), data.at[block], load_sem.at[block]
        )

    def store(block):
        return pltpu.make_async_copy(moved.at[block], moved_out.at[block], store_sem.at[block])

    small = [
        pltpu.make_async_copy(offsets_in, offsets, small_sem.at[0]),
        pltpu.make_async_copy(weights_in, weights, small_sem.at[1]),
        pltpu.make_async_copy(skips_in, skips, small_sem.at[2]),
    ]
    for copy in small:
        copy.start()
    for k in range(half):
        load(k).start()
        load(half + k).start()

    barrier = pltpu.get_barrier_semaphore()

    @pl.loop(1, n)
    def _(by):
        pl.semaphore_signal(
            barrier, inc=1, device_id={"rows": lax.rem(me + by, n)}, device_id_type=MESH
        )

    @pl.when(position > 0)
    def _():
        pl.semaphore_signal(
            barrier, inc=1, device_id={"pairs": position - 1}, device_id_type=MESH
        )

    @pl.when(position < n_pairs - 1)
    def _():
        pl.semaphore_signal(
            barrier, inc=1, device_id={"pairs": position + 1}, device_id_type=MESH
        )

    def give(step, k):
        @pl.loop(0, copies)
        def _(at):
            to = k * copies + at

            @pl.when(to != me)
            def _():
                pltpu.make_async_remote_copy(
                    src_ref=partial.at[step, k],
                    dst_ref=arrived.at[step, me],
                    send_sem=give_sem.at[step],
                    recv_sem=arrive_sem.at[step],
                    device_id={"rows": to},
                    device_id_type=MESH,
                ).start()

            @pl.when(to == me)
            def _():
                arrived[step, me] = partial[step, k]

    def own_coefs(step, shifts):
        some = arrived.at[step, pl.ds(0, n - 1)]
        pltpu.make_async_copy(some, some, arrive_sem.at[step]).wait()
        total = jnp.sum(arrived[step], axis=0)
        coefs[step, own] = turn(total, skips[step, own], shifts)
        target = coefs.at[0] if step == 0 else coefs_out

        @pl.loop(1, half)
        def _(by):
            to = lax.rem(own + by, half) * copies + group
            pltpu.make_async_remote_copy(
                src_ref=coefs.at[step, own],
                dst_ref=target.at[own],
                send_sem=spread_sem.at[step],
                recv_sem=coef_sem.at[step, own],
                device_id={"rows": to},
                device_id_type=MESH,
            ).start()

    def wait_coefs(step, k):
        tile = coefs.at[step, k]

        @pl.when(k != own)
        def _():
            pltpu.make_async_copy(tile, tile, coef_sem.at[step, k]).wait()

    for copy in small:
        copy.wait()
    shifts = shifts_of(offsets, 0)

    def first_products(k):
        load(k).wait()
        load(half + k).wait()
        scale = (weights[pl.ds(k, 1), :], weights[pl.ds(half + k, 1), :])
        products(data.at[k], data.at[half + k], shifts, rows, scale, partial.at[0, k])

    early = half // 2

    @pl.loop(0, early)
    def _(k):
        first_products(k)

    pl.semaphore_wait(barrier, n - 1 + not_first + 1 - is_last)

    @pl.loop(0, early)
    def _(k):
        give(0, k)

    @pl.loop(early, half)
    def _(k):
        first_products(k)
        give(0, k)

    own_coefs(0, shifts)

    def first_turn(k, upper_to, lower_to):
        wait_coefs(0, k)
        rotate(
            data.at[k], data.at[half + k], moved.at[upper_to], moved.at[lower_to],
            coefs.at[0, k], shifts, rows,
        )

    out_low, out_up = 2 * half, 2 * half + 1
    low_zero = (1 - not_first) + out_low * not_first
    up_last = (2 * half - 1) * is_last + out_up * (1 - is_last)
    up_copy = pltpu.make_async_remote_copy(
        src_ref=moved.at[out_up],
        dst_ref=moved.at[0],
        send_sem=pair_sem.at[0],
        recv_sem=pair_sem.at[1],
        device_id={"pairs": lax.rem(position + 1, n_pairs)},
        device_id_type=MESH,
    )
    low_copy = pltpu.make_async_remote_copy(
        src_ref=moved.at[out_low],
        dst_ref=moved.at[2 * half - 1],
        send_sem=pair_sem.at[2],
        recv_sem=pair_sem.at[3],
        device_id={"pairs": lax.rem(position + n_pairs - 1, n_pairs)},
        device_id_type=MESH,
    )

    first_turn(half - 1, up_last, 2 * half - 2)

    @pl.when(position < n_pairs - 1)
    def _():
        up_copy.start()

    first_turn(0, not_first, low_zero)

    @pl.when(position > 0)
    def _():
        low_copy.start()

    @pl.loop(1, half - 1)
    def _(k):
        first_turn(k, k + 1, half + k - 1)

    later = shifts_of(offsets, 1)

    def second_products(k):
        store(k).start()
        store(half + k).start()
        products(moved.at[k], moved.at[half + k], later, rows, None, partial.at[1, k])
        give(1, k)

    @pl.loop(1, half - 1)
    def _(k):
        second_products(k)

    @pl.when(position > 0)
    def _():
        up_copy.wait_recv()

    second_products(0)

    @pl.when(position < n_pairs - 1)
    def _():
        low_copy.wait_recv()

    second_products(half - 1)
    own_coefs(1, later)
    own_copy = pltpu.make_async_copy(coefs.at[1, own], coefs_out.at[own], coef_sem.at[1, own])
    own_copy.start()

    @pl.when(position > 0)
    def _():
        low_copy.wait_send()

    @pl.when(position < n_pairs - 1)
    def _():
        up_copy.wait_send()

    for step in range(STEPS):
        some = arrived.at[step, pl.ds(0, n - 1)]
        pltpu.make_async_copy(some, some, give_sem.at[step]).wait()
        rest = coefs.at[step, pl.ds(0, half - 1)]
        pltpu.make_async_copy(rest, rest, spread_sem.at[step]).wait()

    @pl.loop(0, 2 * half)
    def _(block):
        store(block).wait()

    own_copy.wait()

    @pl.loop(0, half)
    def _(k):
        wait_coefs(1, k)


def last_kernel(
    scale, half, rows,
    moved, coefs_in, offsets,
    rotated, power,
    data, coefs, load_sem, coef_sem, store_sem,
):
    def load(block):
        return pltpu.make_async_copy(moved.at[block], data.at[block], load_sem.at[block])

    def store(block):
        return pltpu.make_async_copy(
            data.at[block], column_block(rotated, block), store_sem.at[block]
        )

    coef_copy = pltpu.make_async_copy(coefs_in, coefs, coef_sem)
    coef_copy.start()
    for k in range(half):
        load(k).start()
        load(half + k).start()
    shifts = shifts_of(offsets, STEPS - 1)
    coef_copy.wait()

    @pl.loop(0, half)
    def _(k):
        load(k).wait()
        load(half + k).wait()
        upper, lower = data.at[k], data.at[half + k]
        rotate(upper, lower, upper, lower, coefs.at[k], shifts, rows)
        store(k).start()
        store(half + k).start()
        power[pl.ds(k, 1), :] = coefs[k, pl.ds(6, 1), :] * scale
        power[pl.ds(half + k, 1), :] = coefs[k, pl.ds(7, 1), :] * scale

    @pl.loop(0, 2 * half)
    def _(block):
        store(block).wait()


def per_device(n, n_pairs, loads, col_weights, partner_offsets, skip_mask):
    rows, columns = loads.shape
    half = columns // (2 * BLOCK)
    tiles = (TILE, BLOCK)
    hbm = pl.BlockSpec(memory_space=pltpu.HBM)
    dma = pltpu.SemaphoreType.DMA
    limit = 60 * 1024 * 1024
    moved, coefs = pl.pallas_call(
        functools.partial(turning_kernel, n, n_pairs, half, rows),
        out_shape=(
            jax.ShapeDtypeStruct((2 * half, rows, BLOCK), jnp.float32),
            jax.ShapeDtypeStruct((half,) + tiles, jnp.float32),
        ),
        in_specs=[hbm] * 4,
        out_specs=(hbm, hbm),
        scratch_shapes=[
            pltpu.VMEM((2 * half, BLOCK), jnp.float32),
            pltpu.SMEM(partner_offsets.shape, jnp.int32),
            pltpu.SMEM(skip_mask.shape, jnp.int32),
            pltpu.VMEM((2 * half, rows, BLOCK), jnp.float32),
            pltpu.VMEM((2 * half + 2, rows, BLOCK), jnp.float32),
            pltpu.VMEM((STEPS, half) + tiles, jnp.float32),
            pltpu.VMEM((STEPS, n) + tiles, jnp.float32),
            pltpu.VMEM((STEPS, half) + tiles, jnp.float32),
            dma((3,)),
            dma((2 * half,)),
            dma((2 * half,)),
            dma((STEPS,)),
            dma((STEPS,)),
            dma((STEPS,)),
            dma((STEPS, half)),
            dma((4,)),
        ],
        compiler_params=pltpu.CompilerParams(
            collective_id=0, has_side_effects=True, vmem_limit_bytes=limit
        ),
        cost_estimate=pl.CostEstimate(
            flops=60 * loads.size, bytes_accessed=8 * loads.size, transcendentals=0
        ),
    )(loads, col_weights.reshape(2 * half, BLOCK), partner_offsets, skip_mask)
    rotated, power = pl.pallas_call(
        functools.partial(last_kernel, 1.0 / (rows * n), half, rows),
        out_shape=(
            jax.ShapeDtypeStruct(loads.shape, jnp.float32),
            jax.ShapeDtypeStruct((2 * half, BLOCK), jnp.float32),
        ),
        in_specs=[hbm, hbm, pl.BlockSpec(memory_space=pltpu.SMEM)],
        out_specs=(hbm, pl.BlockSpec(memory_space=pltpu.VMEM)),
        scratch_shapes=[
            pltpu.VMEM((2 * half, rows, BLOCK), jnp.float32),
            pltpu.VMEM((half,) + tiles, jnp.float32),
            dma((2 * half,)),
            dma(()),
            dma((2 * half,)),
        ],
        compiler_params=pltpu.CompilerParams(vmem_limit_bytes=limit),
        cost_estimate=pl.CostEstimate(
            flops=20 * loads.size, bytes_accessed=8 * loads.size, transcendentals=0
        ),
    )(moved, coefs, partner_offsets)
    return rotated, power.reshape(columns)


def solution(mesh):
    in_specs = (P("rows", "pairs"), P("pairs"), P(), P(None, "pairs"))
    out_specs = (P("rows", "pairs"), P("pairs"))
    return jax.shard_map(
        functools.partial(per_device, mesh.shape["rows"], mesh.shape["pairs"]),
        mesh=mesh, in_specs=in_specs, out_specs=out_specs, check_vma=False,
    )
```

```python
import functools
import jax
import jax.numpy as jnp
from jax import lax
from jax.experimental import pallas as pl
from jax.experimental.pallas import tpu as pltpu
from jax.sharding import PartitionSpec as P

BLOCK = 128
STEPS = 2
TILE = 8
CHUNK = 32
MESH = pl.DeviceIdType.MESH


def rolled(x, shift):
    return pltpu.roll(x, shift, 1)


def fold(x):
    return jnp.sum(x.reshape(x.shape[0] // TILE, TILE, BLOCK), axis=0)


def shifts_of(offsets, step):
    first, second = offsets[step, 0], offsets[step, 1]
    to_first = lax.rem(BLOCK - first, BLOCK)
    to_second = lax.rem(BLOCK - second, BLOCK)
    between = lax.rem(BLOCK + first - second, BLOCK)
    return to_first, to_second, between, second


def permutations(shifts, target):
    to_first, to_second, between, back = shifts
    shape = (2 * BLOCK, BLOCK)
    apart = lax.broadcasted_iota(jnp.int32, shape, 0) - lax.broadcasted_iota(jnp.int32, shape, 1)
    for at, shift in enumerate((between, to_first, to_second, back)):
        hit = lax.rem(apart + (shift + BLOCK), BLOCK) == 0
        target[:, at * BLOCK : (at + 1) * BLOCK] = jnp.where(hit, 1.0, 0.0).astype(jnp.bfloat16)


def put_split(x, target, spot):
    high = x.astype(jnp.bfloat16)
    target[spot, :BLOCK] = high
    target[spot, BLOCK:] = (x - high.astype(jnp.float32)).astype(jnp.bfloat16)


def times(x, matrix):
    return jnp.dot(x, matrix, preferred_element_type=jnp.float32)


def chunks(rows, body, carry):
    def step(at, carry):
        return body(pl.ds(pl.multiple_of(at * CHUNK, CHUNK), CHUNK), carry)

    return lax.fori_loop(0, rows // CHUNK, step, carry, unroll=True)


zero_tile = (TILE, BLOCK)


def roll_all(upper, lower, perms, splits, turned, rows, weights):
    def body(spot, sums):
        u, l = upper[spot, :], lower[spot, :]
        if weights is not None:
            u, l = u * weights[0], l * weights[1]
            upper[spot, :] = u
        put_split(u, splits.at[0], spot)
        put_split(l, splits.at[1], spot)
        return sums[0] + fold(u * u), sums[1] + fold(l * l)

    zero = jnp.zeros(zero_tile, jnp.float32)
    sums = chunks(rows, body, (zero, zero))
    turned[:, :BLOCK] = times(splits[0], perms[:, :BLOCK])
    turned[:, BLOCK:] = times(splits[1], perms[:, BLOCK : 3 * BLOCK])
    return sums


def parts_of(upper, turned, spot):
    lp, ld = turned[spot, BLOCK : 2 * BLOCK], turned[spot, 2 * BLOCK :]
    return upper[spot, :], lp, turned[spot, :BLOCK], ld


def products(upper, lower, perms, splits, turned, rows, weights, partial):
    squares = roll_all(upper, lower, perms, splits, turned, rows, weights)

    def body(spot, sums):
        u, lp, ud, ld = parts_of(upper, turned, spot)
        pairs = ((u, lp), (u, ud), (u, ld), (lp, ud), (lp, ld))
        return tuple(total + fold(a * b) for total, (a, b) in zip(sums, pairs))

    zero = jnp.zeros(zero_tile, jnp.float32)
    sums = squares + chunks(rows, body, (zero,) * 5)
    for at, total in enumerate(sums):
        partial[pl.ds(at, 1), :] = jnp.sum(total, axis=0, keepdims=True)
    partial[pl.ds(7, 1), :] = jnp.zeros((1, BLOCK), jnp.float32)


def angle(a, b, g):
    half_gap = 0.5 * (b - a)
    sign = jnp.where(half_gap >= 0.0, 1.0, -1.0)
    denominator = jnp.maximum(
        jnp.abs(half_gap) + jnp.sqrt(half_gap * half_gap + g * g), 1e-06 * (a + b)
    )
    t = sign * g / denominator
    c = 1.0 / jnp.sqrt(1.0 + t * t)
    return c, t * c


def norms(a, b, g, c, s):
    cross = 2.0 * c * s * g
    return c * c * a - cross + s * s * b, s * s * a + cross + c * c * b


def turn(total, skip, shifts):
    to_first, _, between, back = shifts
    row = [jnp.broadcast_to(total[at : at + 1, :], (TILE, BLOCK)) for at in range(7)]
    a, b, g, u_ud, u_ld, l_ud, l_ld = row
    b = rolled(b, to_first)
    keep = jnp.full((TILE, BLOCK), skip, jnp.int32) == 0
    c, s = angle(a, b, g)
    c, s = jnp.where(keep, c, 1.0), jnp.where(keep, s, 0.0)
    a1, b1 = norms(a, b, g, c, s)
    cd, sd, bd = rolled(c, between), rolled(s, between), rolled(b1, between)
    g1 = c * (sd * u_ud + cd * u_ld) - s * (sd * l_ud + cd * l_ld)
    c2, s2 = angle(a1, bd, g1)
    c2, s2 = jnp.where(keep, c2, 1.0), jnp.where(keep, s2, 0.0)
    a2, b2 = norms(a1, bd, g1, c2, s2)
    place = lax.broadcasted_iota(jnp.int32, (TILE, BLOCK), 0)
    tile = rolled(b2, back)
    for at, value in enumerate((c, s, cd, sd, c2, s2, a2)):
        tile = jnp.where(place == at, value, tile)
    return tile


def rotate(upper, new_upper, new_lower, coefs, perms, splits, turned, rows):
    tile = coefs[...]
    c, s, cd, sd, c2, s2 = (tile[at : at + 1, :] for at in range(6))
    up = (c2 * c, -c2 * s, -s2 * sd, -s2 * cd)
    low = (s2 * c, -s2 * s, c2 * sd, c2 * cd)

    def body(spot, carry):
        parts = parts_of(upper, turned, spot)
        new_upper[spot, :] = sum(f * x for f, x in zip(up, parts))
        put_split(sum(f * x for f, x in zip(low, parts)), splits.at[1], spot)
        return carry

    chunks(rows, body, 0)
    new_lower[...] = times(splits[1], perms[:, 3 * BLOCK :])


def column_block(array, block):
    return array.at[:, pl.ds(pl.multiple_of(block * BLOCK, BLOCK), BLOCK)]


def turning_kernel(
    n, n_pairs, half, rows,
    loads, weights_in, offsets_in, skips_in,
    moved_out, coefs_out,
    weights, offsets, skips, data, moved, partial, arrived, coefs, perms, splits, turned,
    small_sem, load_sem, store_sem, give_sem, arrive_sem, spread_sem, coef_sem, pair_sem,
):
    me, position = lax.axis_index("rows"), lax.axis_index("pairs")
    copies = n // half
    own, group = me // copies, lax.rem(me, copies)
    not_first = (position + n_pairs - 1) // n_pairs
    is_last = (position + 1) // n_pairs

    def load(block):
        return pltpu.make_async_copy(
            column_block(loads, block), data.at[block], load_sem.at[block]
        )

    def store(block):
        return pltpu.make_async_copy(moved.at[block], moved_out.at[block], store_sem.at[block])

    small = [
        pltpu.make_async_copy(offsets_in, offsets, small_sem.at[0]),
        pltpu.make_async_copy(weights_in, weights, small_sem.at[1]),
        pltpu.make_async_copy(skips_in, skips, small_sem.at[2]),
    ]
    for copy in small:
        copy.start()
    for k in range(half):
        load(k).start()
        load(half + k).start()

    barrier = pltpu.get_barrier_semaphore()

    @pl.loop(1, n)
    def _(by):
        pl.semaphore_signal(
            barrier, inc=1, device_id={"rows": lax.rem(me + by, n)}, device_id_type=MESH
        )

    @pl.when(position > 0)
    def _():
        pl.semaphore_signal(
            barrier, inc=1, device_id={"pairs": position - 1}, device_id_type=MESH
        )

    @pl.when(position < n_pairs - 1)
    def _():
        pl.semaphore_signal(
            barrier, inc=1, device_id={"pairs": position + 1}, device_id_type=MESH
        )

    def give(step, k):
        @pl.loop(0, copies)
        def _(at):
            to = k * copies + at

            @pl.when(to != me)
            def _():
                pltpu.make_async_remote_copy(
                    src_ref=partial.at[step, k],
                    dst_ref=arrived.at[step, me],
                    send_sem=give_sem.at[step],
                    recv_sem=arrive_sem.at[step],
                    device_id={"rows": to},
                    device_id_type=MESH,
                ).start()

            @pl.when(to == me)
            def _():
                arrived[step, me] = partial[step, k]

    def own_coefs(step, shifts):
        some = arrived.at[step, pl.ds(0, n - 1)]
        pltpu.make_async_copy(some, some, arrive_sem.at[step]).wait()
        total = jnp.sum(arrived[step], axis=0)
        coefs[step, own] = turn(total, skips[step, own], shifts)
        target = coefs.at[0] if step == 0 else coefs_out

        @pl.loop(1, half)
        def _(by):
            to = lax.rem(own + by, half) * copies + group
            pltpu.make_async_remote_copy(
                src_ref=coefs.at[step, own],
                dst_ref=target.at[own],
                send_sem=spread_sem.at[step],
                recv_sem=coef_sem.at[step, own],
                device_id={"rows": to},
                device_id_type=MESH,
            ).start()

    def wait_coefs(step, k):
        tile = coefs.at[step, k]

        @pl.when(k != own)
        def _():
            pltpu.make_async_copy(tile, tile, coef_sem.at[step, k]).wait()

    for copy in small:
        copy.wait()
    shifts = shifts_of(offsets, 0)
    later = shifts_of(offsets, 1)
    permutations(shifts, perms.at[0])

    def first_products(k):
        load(k).wait()
        load(half + k).wait()
        scale = (weights[pl.ds(k, 1), :], weights[pl.ds(half + k, 1), :])
        products(
            data.at[k], data.at[half + k], perms.at[0], splits.at[k], turned.at[k],
            rows, scale, partial.at[0, k],
        )

    early = half // 2

    @pl.loop(0, early)
    def _(k):
        first_products(k)

    pl.semaphore_wait(barrier, n - 1 + not_first + 1 - is_last)

    @pl.loop(0, early)
    def _(k):
        give(0, k)

    @pl.loop(early, half)
    def _(k):
        first_products(k)
        give(0, k)

    permutations(later, perms.at[1])
    own_coefs(0, shifts)

    def first_turn(k, upper_to, lower_to):
        wait_coefs(0, k)
        rotate(
            data.at[k], moved.at[upper_to], moved.at[lower_to], coefs.at[0, k],
            perms.at[0], splits.at[k], turned.at[k], rows,
        )

    out_low, out_up = 2 * half, 2 * half + 1
    low_zero = (1 - not_first) + out_low * not_first
    up_last = (2 * half - 1) * is_last + out_up * (1 - is_last)
    up_copy = pltpu.make_async_remote_copy(
        src_ref=moved.at[out_up],
        dst_ref=moved.at[0],
        send_sem=pair_sem.at[0],
        recv_sem=pair_sem.at[1],
        device_id={"pairs": lax.rem(position + 1, n_pairs)},
        device_id_type=MESH,
    )
    low_copy = pltpu.make_async_remote_copy(
        src_ref=moved.at[out_low],
        dst_ref=moved.at[2 * half - 1],
        send_sem=pair_sem.at[2],
        recv_sem=pair_sem.at[3],
        device_id={"pairs": lax.rem(position + n_pairs - 1, n_pairs)},
        device_id_type=MESH,
    )

    first_turn(half - 1, up_last, 2 * half - 2)

    @pl.when(position < n_pairs - 1)
    def _():
        up_copy.start()

    first_turn(0, not_first, low_zero)

    @pl.when(position > 0)
    def _():
        low_copy.start()

    @pl.loop(1, half - 1)
    def _(k):
        first_turn(k, k + 1, half + k - 1)

    def second_products(k):
        store(k).start()
        store(half + k).start()
        products(
            moved.at[k], moved.at[half + k], perms.at[1], splits.at[k], turned.at[k],
            rows, None, partial.at[1, k],
        )
        give(1, k)

    @pl.loop(1, half - 1)
    def _(k):
        second_products(k)

    @pl.when(position > 0)
    def _():
        up_copy.wait_recv()

    second_products(0)

    @pl.when(position < n_pairs - 1)
    def _():
        low_copy.wait_recv()

    second_products(half - 1)
    own_coefs(1, later)
    own_copy = pltpu.make_async_copy(coefs.at[1, own], coefs_out.at[own], coef_sem.at[1, own])
    own_copy.start()

    @pl.when(position > 0)
    def _():
        low_copy.wait_send()

    @pl.when(position < n_pairs - 1)
    def _():
        up_copy.wait_send()

    for step in range(STEPS):
        some = arrived.at[step, pl.ds(0, n - 1)]
        pltpu.make_async_copy(some, some, give_sem.at[step]).wait()
        rest = coefs.at[step, pl.ds(0, half - 1)]
        pltpu.make_async_copy(rest, rest, spread_sem.at[step]).wait()

    @pl.loop(0, 2 * half)
    def _(block):
        store(block).wait()

    own_copy.wait()

    @pl.loop(0, half)
    def _(k):
        wait_coefs(1, k)


def last_kernel(
    scale, half, rows,
    moved, coefs_in, offsets,
    rotated, power,
    data, coefs, perms, splits, turned, load_sem, coef_sem, store_sem,
):
    def load(block):
        return pltpu.make_async_copy(moved.at[block], data.at[block], load_sem.at[block])

    def store(block):
        return pltpu.make_async_copy(
            data.at[block], column_block(rotated, block), store_sem.at[block]
        )

    coef_copy = pltpu.make_async_copy(coefs_in, coefs, coef_sem)
    coef_copy.start()
    for k in range(half):
        load(k).start()
        load(half + k).start()
    permutations(shifts_of(offsets, STEPS - 1), perms)
    coef_copy.wait()

    @pl.loop(0, half)
    def _(k):
        load(k).wait()
        load(half + k).wait()
        upper, lower = data.at[k], data.at[half + k]
        roll_all(upper, lower, perms, splits.at[k], turned.at[k], rows, None)
        rotate(
            upper, upper, lower, coefs.at[k], perms, splits.at[k], turned.at[k], rows
        )
        store(k).start()
        store(half + k).start()
        power[pl.ds(k, 1), :] = coefs[k, pl.ds(6, 1), :] * scale
        power[pl.ds(half + k, 1), :] = coefs[k, pl.ds(7, 1), :] * scale

    @pl.loop(0, 2 * half)
    def _(block):
        store(block).wait()


def per_device(n, n_pairs, loads, col_weights, partner_offsets, skip_mask):
    rows, columns = loads.shape
    half = columns // (2 * BLOCK)
    tiles = (TILE, BLOCK)
    hbm = pl.BlockSpec(memory_space=pltpu.HBM)
    dma = pltpu.SemaphoreType.DMA
    limit = 60 * 1024 * 1024
    moved, coefs = pl.pallas_call(
        functools.partial(turning_kernel, n, n_pairs, half, rows),
        out_shape=(
            jax.ShapeDtypeStruct((2 * half, rows, BLOCK), jnp.float32),
            jax.ShapeDtypeStruct((half,) + tiles, jnp.float32),
        ),
        in_specs=[hbm] * 4,
        out_specs=(hbm, hbm),
        scratch_shapes=[
            pltpu.VMEM((2 * half, BLOCK), jnp.float32),
            pltpu.SMEM(partner_offsets.shape, jnp.int32),
            pltpu.SMEM(skip_mask.shape, jnp.int32),
            pltpu.VMEM((2 * half, rows, BLOCK), jnp.float32),
            pltpu.VMEM((2 * half + 2, rows, BLOCK), jnp.float32),
            pltpu.VMEM((STEPS, half) + tiles, jnp.float32),
            pltpu.VMEM((STEPS, n) + tiles, jnp.float32),
            pltpu.VMEM((STEPS, half) + tiles, jnp.float32),
            pltpu.VMEM((STEPS, 2 * BLOCK, 4 * BLOCK), jnp.bfloat16),
            pltpu.VMEM((half, 2, rows, 2 * BLOCK), jnp.bfloat16),
            pltpu.VMEM((half, rows, 3 * BLOCK), jnp.float32),
            dma((3,)),
            dma((2 * half,)),
            dma((2 * half,)),
            dma((STEPS,)),
            dma((STEPS,)),
            dma((STEPS,)),
            dma((STEPS, half)),
            dma((4,)),
        ],
        compiler_params=pltpu.CompilerParams(
            collective_id=0, has_side_effects=True, vmem_limit_bytes=limit
        ),
        cost_estimate=pl.CostEstimate(
            flops=60 * loads.size, bytes_accessed=8 * loads.size, transcendentals=0
        ),
    )(loads, col_weights.reshape(2 * half, BLOCK), partner_offsets, skip_mask)
    rotated, power = pl.pallas_call(
        functools.partial(last_kernel, 1.0 / (rows * n), half, rows),
        out_shape=(
            jax.ShapeDtypeStruct(loads.shape, jnp.float32),
            jax.ShapeDtypeStruct((2 * half, BLOCK), jnp.float32),
        ),
        in_specs=[hbm, hbm, pl.BlockSpec(memory_space=pltpu.SMEM)],
        out_specs=(hbm, pl.BlockSpec(memory_space=pltpu.VMEM)),
        scratch_shapes=[
            pltpu.VMEM((2 * half, rows, BLOCK), jnp.float32),
            pltpu.VMEM((half,) + tiles, jnp.float32),
            pltpu.VMEM((2 * BLOCK, 4 * BLOCK), jnp.bfloat16),
            pltpu.VMEM((half, 2, rows, 2 * BLOCK), jnp.bfloat16),
            pltpu.VMEM((half, rows, 3 * BLOCK), jnp.float32),
            dma((2 * half,)),
            dma(()),
            dma((2 * half,)),
        ],
        compiler_params=pltpu.CompilerParams(vmem_limit_bytes=limit),
        cost_estimate=pl.CostEstimate(
            flops=20 * loads.size, bytes_accessed=8 * loads.size, transcendentals=0
        ),
    )(moved, coefs, partner_offsets)
    return rotated, power.reshape(columns)


def solution(mesh):
    in_specs = (P("rows", "pairs"), P("pairs"), P(), P(None, "pairs"))
    out_specs = (P("rows", "pairs"), P("pairs"))
    return jax.shard_map(
        functools.partial(per_device, mesh.shape["rows"], mesh.shape["pairs"]),
        mesh=mesh, in_specs=in_specs, out_specs=out_specs, check_vma=False,
    )
```

```python
import functools
import jax
import jax.numpy as jnp
from jax import lax
from jax.experimental import pallas as pl
from jax.experimental.pallas import tpu as pltpu
from jax.sharding import PartitionSpec as P

BLOCK = 128
STEPS = 2
TILE = 8
CHUNK = 32
MESH = pl.DeviceIdType.MESH


def rolled(x, shift):
    return pltpu.roll(x, shift, 1)


def fold(x):
    return jnp.sum(x.reshape(x.shape[0] // TILE, TILE, BLOCK), axis=0)


def shifts_of(offsets, step):
    first, second = offsets[step, 0], offsets[step, 1]
    to_first = lax.rem(BLOCK - first, BLOCK)
    to_second = lax.rem(BLOCK - second, BLOCK)
    between = lax.rem(BLOCK + first - second, BLOCK)
    return to_first, to_second, between, second


def chunks(rows, body, carry):
    def step(at, carry):
        return body(pl.ds(pl.multiple_of(at * CHUNK, CHUNK), CHUNK), carry)

    return lax.fori_loop(0, rows // CHUNK, step, carry, unroll=True)


def products(upper, lower, shifts, turned, rows, partial):
    to_first, to_second, between, _ = shifts

    def body(spot, sums):
        u, l = upper[spot, :], lower[spot, :]
        lp, ud, ld = rolled(l, to_first), rolled(u, between), rolled(l, to_second)
        for at, x in enumerate((lp, ud, ld)):
            turned[at, spot, :] = x
        pairs = ((u, u), (l, l), (u, lp), (u, ud), (u, ld), (lp, ud), (lp, ld))
        return tuple(total + fold(a * b) for total, (a, b) in zip(sums, pairs))

    zero = jnp.zeros((TILE, BLOCK), jnp.float32)
    sums = chunks(rows, body, (zero,) * 7)
    for at, total in enumerate(sums):
        partial[pl.ds(at, 1), :] = jnp.sum(total, axis=0, keepdims=True)
    partial[pl.ds(7, 1), :] = jnp.zeros((1, BLOCK), jnp.float32)


def angle(a, b, g):
    half_gap = 0.5 * (b - a)
    sign = jnp.where(half_gap >= 0.0, 1.0, -1.0)
    denominator = jnp.maximum(
        jnp.abs(half_gap) + jnp.sqrt(half_gap * half_gap + g * g), 1e-06 * (a + b)
    )
    t = sign * g / denominator
    c = 1.0 / jnp.sqrt(1.0 + t * t)
    return c, t * c


def norms(a, b, g, c, s):
    cross = 2.0 * c * s * g
    return c * c * a - cross + s * s * b, s * s * a + cross + c * c * b


def turn(total, skip, shifts):
    to_first, _, between, back = shifts
    row = [jnp.broadcast_to(total[at : at + 1, :], (TILE, BLOCK)) for at in range(7)]
    a, b, g, u_ud, u_ld, l_ud, l_ld = row
    b = rolled(b, to_first)
    keep = jnp.full((TILE, BLOCK), skip, jnp.int32) == 0
    c, s = angle(a, b, g)
    c, s = jnp.where(keep, c, 1.0), jnp.where(keep, s, 0.0)
    a1, b1 = norms(a, b, g, c, s)
    cd, sd, bd = rolled(c, between), rolled(s, between), rolled(b1, between)
    g1 = c * (sd * u_ud + cd * u_ld) - s * (sd * l_ud + cd * l_ld)
    c2, s2 = angle(a1, bd, g1)
    c2, s2 = jnp.where(keep, c2, 1.0), jnp.where(keep, s2, 0.0)
    a2, b2 = norms(a1, bd, g1, c2, s2)
    place = lax.broadcasted_iota(jnp.int32, (TILE, BLOCK), 0)
    tile = rolled(b2, back)
    for at, value in enumerate((c, s, cd, sd, c2, s2, a2)):
        tile = jnp.where(place == at, value, tile)
    return tile


def rotate(upper, new_upper, new_lower, coefs, back, turned, rows):
    tile = coefs[...]
    c, s, cd, sd, c2, s2 = (tile[at : at + 1, :] for at in range(6))
    up = (c2 * c, -c2 * s, -s2 * sd, -s2 * cd)
    low = (s2 * c, -s2 * s, c2 * sd, c2 * cd)

    def body(spot, carry):
        parts = [upper[spot, :]] + [turned[at, spot, :] for at in range(3)]
        new_upper[spot, :] = sum(f * x for f, x in zip(up, parts))
        new_lower[spot, :] = rolled(sum(f * x for f, x in zip(low, parts)), back)
        return carry

    chunks(rows, body, 0)


def column_block(array, block):
    return array.at[:, pl.ds(pl.multiple_of(block * BLOCK, BLOCK), BLOCK)]


def turning_kernel(
    n, n_pairs, half, rows,
    data, offsets, skips,
    rotated, power,
    moved, partial, arrived, coefs, turned,
    give_sem, arrive_sem, spread_sem, coef_sem, pair_sem,
):
    me, position = lax.axis_index("rows"), lax.axis_index("pairs")
    copies = n // half
    own, group = me // copies, lax.rem(me, copies)
    not_first = (position + n_pairs - 1) // n_pairs
    is_last = (position + 1) // n_pairs

    barrier = pltpu.get_barrier_semaphore()

    @pl.loop(1, n)
    def _(by):
        pl.semaphore_signal(
            barrier, inc=1, device_id={"rows": lax.rem(me + by, n)}, device_id_type=MESH
        )

    @pl.when(position > 0)
    def _():
        pl.semaphore_signal(
            barrier, inc=1, device_id={"pairs": position - 1}, device_id_type=MESH
        )

    @pl.when(position < n_pairs - 1)
    def _():
        pl.semaphore_signal(
            barrier, inc=1, device_id={"pairs": position + 1}, device_id_type=MESH
        )

    def give(step, k):
        @pl.loop(0, copies)
        def _(at):
            to = k * copies + at

            @pl.when(to != me)
            def _():
                pltpu.make_async_remote_copy(
                    src_ref=partial.at[step, k],
                    dst_ref=arrived.at[step, me],
                    send_sem=give_sem.at[step],
                    recv_sem=arrive_sem.at[step],
                    device_id={"rows": to},
                    device_id_type=MESH,
                ).start()

            @pl.when(to == me)
            def _():
                arrived[step, me] = partial[step, k]

    def own_coefs(step, shifts):
        some = arrived.at[step, pl.ds(0, n - 1)]
        pltpu.make_async_copy(some, some, arrive_sem.at[step]).wait()
        total = jnp.sum(arrived[step], axis=0)
        coefs[step, own] = turn(total, skips[step, own], shifts)

        @pl.loop(1, half)
        def _(by):
            to = lax.rem(own + by, half) * copies + group
            pltpu.make_async_remote_copy(
                src_ref=coefs.at[step, own],
                dst_ref=coefs.at[step, own],
                send_sem=spread_sem.at[step],
                recv_sem=coef_sem.at[step, own],
                device_id={"rows": to},
                device_id_type=MESH,
            ).start()

    def wait_coefs(step, k):
        tile = coefs.at[step, k]

        @pl.when(k != own)
        def _():
            pltpu.make_async_copy(tile, tile, coef_sem.at[step, k]).wait()

    shifts, later = shifts_of(offsets, 0), shifts_of(offsets, 1)

    def first_products(k):
        products(
            column_block(data, k), column_block(data, half + k), shifts, turned.at[k],
            rows, partial.at[0, k],
        )

    early = half // 2

    @pl.loop(0, early)
    def _(k):
        first_products(k)

    pl.semaphore_wait(barrier, n - 1 + not_first + 1 - is_last)

    @pl.loop(0, early)
    def _(k):
        give(0, k)

    @pl.loop(early, half)
    def _(k):
        first_products(k)
        give(0, k)

    own_coefs(0, shifts)

    def first_turn(k, upper_to, lower_to):
        wait_coefs(0, k)
        rotate(
            column_block(data, k), moved.at[upper_to], moved.at[lower_to],
            coefs.at[0, k], shifts[3], turned.at[k], rows,
        )

    out_low, out_up = 2 * half, 2 * half + 1
    low_zero = (1 - not_first) + out_low * not_first
    up_last = (2 * half - 1) * is_last + out_up * (1 - is_last)
    up_copy = pltpu.make_async_remote_copy(
        src_ref=moved.at[out_up],
        dst_ref=moved.at[0],
        send_sem=pair_sem.at[0],
        recv_sem=pair_sem.at[1],
        device_id={"pairs": lax.rem(position + 1, n_pairs)},
        device_id_type=MESH,
    )
    low_copy = pltpu.make_async_remote_copy(
        src_ref=moved.at[out_low],
        dst_ref=moved.at[2 * half - 1],
        send_sem=pair_sem.at[2],
        recv_sem=pair_sem.at[3],
        device_id={"pairs": lax.rem(position + n_pairs - 1, n_pairs)},
        device_id_type=MESH,
    )

    first_turn(half - 1, up_last, 2 * half - 2)

    @pl.when(position < n_pairs - 1)
    def _():
        up_copy.start()

    first_turn(0, not_first, low_zero)

    @pl.when(position > 0)
    def _():
        low_copy.start()

    @pl.loop(1, half - 1)
    def _(k):
        first_turn(k, k + 1, half + k - 1)

    def second_products(k):
        products(
            moved.at[k], moved.at[half + k], later, turned.at[k], rows, partial.at[1, k]
        )
        give(1, k)

    @pl.loop(1, half - 1)
    def _(k):
        second_products(k)

    @pl.when(position > 0)
    def _():
        up_copy.wait_recv()

    second_products(0)

    @pl.when(position < n_pairs - 1)
    def _():
        low_copy.wait_recv()

    second_products(half - 1)
    own_coefs(1, later)

    @pl.loop(0, half)
    def _(k):
        wait_coefs(1, k)
        rotate(
            moved.at[k], column_block(rotated, k), column_block(rotated, half + k),
            coefs.at[1, k], later[3], turned.at[k], rows,
        )
        tile = coefs[1, k] * (1.0 / (rows * n))
        power[pl.ds(k, 1), :] = tile[6:7, :]
        power[pl.ds(half + k, 1), :] = tile[7:8, :]

    @pl.when(position > 0)
    def _():
        low_copy.wait_send()

    @pl.when(position < n_pairs - 1)
    def _():
        up_copy.wait_send()

    for step in range(STEPS):
        some = arrived.at[step, pl.ds(0, n - 1)]
        pltpu.make_async_copy(some, some, give_sem.at[step]).wait()
        rest = coefs.at[step, pl.ds(0, half - 1)]
        pltpu.make_async_copy(rest, rest, spread_sem.at[step]).wait()


def per_device(n, n_pairs, loads, col_weights, partner_offsets, skip_mask):
    rows, columns = loads.shape
    half = columns // (2 * BLOCK)
    tiles = (TILE, BLOCK)
    vmem = pl.BlockSpec(memory_space=pltpu.VMEM)
    smem = pl.BlockSpec(memory_space=pltpu.SMEM)
    dma = pltpu.SemaphoreType.DMA
    weighted = loads * col_weights[None, :]
    rotated, power = pl.pallas_call(
        functools.partial(turning_kernel, n, n_pairs, half, rows),
        out_shape=(
            jax.ShapeDtypeStruct(loads.shape, jnp.float32),
            jax.ShapeDtypeStruct((2 * half, BLOCK), jnp.float32),
        ),
        in_specs=[vmem, smem, smem],
        out_specs=(vmem, vmem),
        scratch_shapes=[
            pltpu.VMEM((2 * half + 2, rows, BLOCK), jnp.float32),
            pltpu.VMEM((STEPS, half) + tiles, jnp.float32),
            pltpu.VMEM((STEPS, n) + tiles, jnp.float32),
            pltpu.VMEM((STEPS, half) + tiles, jnp.float32),
            pltpu.VMEM((half, 3, rows, BLOCK), jnp.float32),
            dma((STEPS,)),
            dma((STEPS,)),
            dma((STEPS,)),
            dma((STEPS, half)),
            dma((4,)),
        ],
        compiler_params=pltpu.CompilerParams(
            collective_id=0, has_side_effects=True, vmem_limit_bytes=24 * 1024 * 1024
        ),
        cost_estimate=pl.CostEstimate(
            flops=60 * loads.size, bytes_accessed=8 * loads.size, transcendentals=0
        ),
    )(weighted, partner_offsets, skip_mask)
    return rotated, power.reshape(columns)


def solution(mesh):
    in_specs = (P("rows", "pairs"), P("pairs"), P(), P(None, "pairs"))
    out_specs = (P("rows", "pairs"), P("pairs"))
    return jax.shard_map(
        functools.partial(per_device, mesh.shape["rows"], mesh.shape["pairs"]),
        mesh=mesh, in_specs=in_specs, out_specs=out_specs, check_vma=False,
    )
```

```python
import functools
import jax
import jax.numpy as jnp
from jax import lax
from jax.experimental import pallas as pl
from jax.experimental.pallas import tpu as pltpu
from jax.sharding import PartitionSpec as P

BLOCK = 128
STEPS = 2
TILE = 8
CHUNK = 32
MESH = pl.DeviceIdType.MESH


def rolled(x, shift):
    return pltpu.roll(x, shift, 1)


def fold(x):
    return jnp.sum(x.reshape(x.shape[0] // TILE, TILE, BLOCK), axis=0)


def shifts_of(offsets, step):
    first, second = offsets[step, 0], offsets[step, 1]
    to_first = lax.rem(BLOCK - first, BLOCK)
    to_second = lax.rem(BLOCK - second, BLOCK)
    between = lax.rem(BLOCK + first - second, BLOCK)
    return to_first, to_second, between, second


def chunks(rows, body, carry):
    def step(at, carry):
        return body(pl.ds(pl.multiple_of(at * CHUNK, CHUNK), CHUNK), carry)

    return lax.fori_loop(0, rows // CHUNK, step, carry, unroll=True)


def products(upper, lower, shifts, turned, rows, partial):
    to_first, to_second, between, _ = shifts

    def body(spot, sums):
        u, l = upper[spot, :], lower[spot, :]
        lp, ud, ld = rolled(l, to_first), rolled(u, between), rolled(l, to_second)
        for at, x in enumerate((lp, ud, ld)):
            turned[at, spot, :] = x
        pairs = ((u, u), (l, l), (u, lp), (u, ud), (u, ld), (lp, ud), (lp, ld))
        return tuple(total + fold(a * b) for total, (a, b) in zip(sums, pairs))

    zero = jnp.zeros((TILE, BLOCK), jnp.float32)
    sums = chunks(rows, body, (zero,) * 7)
    for at, total in enumerate(sums):
        partial[pl.ds(at, 1), :] = jnp.sum(total, axis=0, keepdims=True)
    partial[pl.ds(7, 1), :] = jnp.zeros((1, BLOCK), jnp.float32)


def angle(a, b, g):
    half_gap = 0.5 * (b - a)
    sign = jnp.where(half_gap >= 0.0, 1.0, -1.0)
    denominator = jnp.maximum(
        jnp.abs(half_gap) + jnp.sqrt(half_gap * half_gap + g * g), 1e-06 * (a + b)
    )
    t = sign * g / denominator
    c = 1.0 / jnp.sqrt(1.0 + t * t)
    return c, t * c


def norms(a, b, g, c, s):
    cross = 2.0 * c * s * g
    return c * c * a - cross + s * s * b, s * s * a + cross + c * c * b


def turn(total, skip, shifts):
    to_first, _, between, back = shifts
    row = [jnp.broadcast_to(total[at : at + 1, :], (TILE, BLOCK)) for at in range(7)]
    a, b, g, u_ud, u_ld, l_ud, l_ld = row
    b = rolled(b, to_first)
    keep = jnp.full((TILE, BLOCK), skip, jnp.int32) == 0
    c, s = angle(a, b, g)
    c, s = jnp.where(keep, c, 1.0), jnp.where(keep, s, 0.0)
    a1, b1 = norms(a, b, g, c, s)
    cd, sd, bd = rolled(c, between), rolled(s, between), rolled(b1, between)
    g1 = c * (sd * u_ud + cd * u_ld) - s * (sd * l_ud + cd * l_ld)
    c2, s2 = angle(a1, bd, g1)
    c2, s2 = jnp.where(keep, c2, 1.0), jnp.where(keep, s2, 0.0)
    a2, b2 = norms(a1, bd, g1, c2, s2)
    place = lax.broadcasted_iota(jnp.int32, (TILE, BLOCK), 0)
    tile = rolled(b2, back)
    for at, value in enumerate((c, s, cd, sd, c2, s2, a2)):
        tile = jnp.where(place == at, value, tile)
    return tile


def rotate(upper, new_upper, new_lower, coefs, back, turned, rows):
    tile = coefs[...]
    c, s, cd, sd, c2, s2 = (tile[at : at + 1, :] for at in range(6))
    up = (c2 * c, -c2 * s, -s2 * sd, -s2 * cd)
    low = (s2 * c, -s2 * s, c2 * sd, c2 * cd)

    def body(spot, carry):
        parts = [upper[spot, :]] + [turned[at, spot, :] for at in range(3)]
        new_upper[spot, :] = sum(f * x for f, x in zip(up, parts))
        new_lower[spot, :] = rolled(sum(f * x for f, x in zip(low, parts)), back)
        return carry

    chunks(rows, body, 0)


def inner_size(half):
    return 4 if half % 4 == 0 else 2


def column_block(array, block):
    return array.at[:, pl.ds(pl.multiple_of(block * BLOCK, BLOCK), BLOCK)]


def turning_kernel(
    n, n_pairs, half, rows,
    data, offsets, skips,
    rotated, power,
    moved, partial, near_parts, far_parts, coefs, turned,
    give_sem, near_sem, pass_sem, far_sem, spread_sem, coef_sem, pair_sem,
):
    me, position = lax.axis_index("rows"), lax.axis_index("pairs")
    near, share = inner_size(half), half // inner_size(half)
    far = n // near
    mine, line = lax.rem(me, near), me // near
    not_first = (position + n_pairs - 1) // n_pairs
    is_last = (position + 1) // n_pairs

    barrier = pltpu.get_barrier_semaphore()

    def near_device(by):
        return line * near + lax.rem(mine + by, near)

    def far_device(by):
        return lax.rem(line + by, far) * near + mine

    def greet(to):
        pl.semaphore_signal(barrier, inc=1, device_id={"rows": to}, device_id_type=MESH)

    for by in range(1, near):
        greet(near_device(by))
    for by in range(1, far):
        greet(far_device(by))

    @pl.when(position > 0)
    def _():
        pl.semaphore_signal(
            barrier, inc=1, device_id={"pairs": position - 1}, device_id_type=MESH
        )

    @pl.when(position < n_pairs - 1)
    def _():
        pl.semaphore_signal(
            barrier, inc=1, device_id={"pairs": position + 1}, device_id_type=MESH
        )

    def pairs_of(at):
        return pl.ds(at * share, share)

    def send(source, target, to, sent, came):
        return pltpu.make_async_remote_copy(
            src_ref=source, dst_ref=target, send_sem=sent, recv_sem=came,
            device_id={"rows": to}, device_id_type=MESH,
        )

    def wait_bytes(ref, sem):
        pltpu.make_async_copy(ref, ref, sem).wait()

    def give(step, at):
        @pl.when(mine != at)
        def _():
            send(
                partial.at[step, pairs_of(at)], near_parts.at[step, mine], line * near + at,
                give_sem.at[step], near_sem.at[step],
            ).start()

    def all_coefs(step, shifts):
        near_parts[step, mine] = partial[step, pairs_of(mine)]
        wait_bytes(near_parts.at[step, pl.ds(0, near - 1)], near_sem.at[step])
        far_parts[step, line] = jnp.sum(near_parts[step], axis=0)
        for by in range(1, far):
            own = far_parts.at[step, line]
            send(own, own, far_device(by), pass_sem.at[step], far_sem.at[step]).start()
        wait_bytes(far_parts.at[step, pl.ds(0, far - 1)], far_sem.at[step])
        total = jnp.sum(far_parts[step], axis=0)
        for at in range(share):
            k = mine * share + at
            coefs[step, k] = turn(total[at], skips[step, k], shifts)
        for by in range(1, near):
            own = coefs.at[step, pairs_of(mine)]
            send(own, own, near_device(by), spread_sem.at[step], coef_sem.at[step]).start()
        wait_bytes(coefs.at[step, pl.ds(0, (near - 1) * share)], coef_sem.at[step])

    shifts, later = shifts_of(offsets, 0), shifts_of(offsets, 1)

    def first_products(k):
        products(
            column_block(data, k), column_block(data, half + k), shifts, turned.at[k],
            rows, partial.at[0, k],
        )

    @pl.loop(0, share)
    def _(k):
        first_products(k)

    pl.semaphore_wait(barrier, near + far - 2 + not_first + 1 - is_last)
    give(0, 0)

    @pl.loop(1, near)
    def _(at):
        @pl.loop(at * share, (at + 1) * share)
        def _(k):
            first_products(k)

        give(0, at)

    all_coefs(0, shifts)

    def first_turn(k, upper_to, lower_to):
        rotate(
            column_block(data, k), moved.at[upper_to], moved.at[lower_to],
            coefs.at[0, k], shifts[3], turned.at[k], rows,
        )

    out_low, out_up = 2 * half, 2 * half + 1
    low_zero = (1 - not_first) + out_low * not_first
    up_last = (2 * half - 1) * is_last + out_up * (1 - is_last)
    up_copy = pltpu.make_async_remote_copy(
        src_ref=moved.at[out_up],
        dst_ref=moved.at[0],
        send_sem=pair_sem.at[0],
        recv_sem=pair_sem.at[1],
        device_id={"pairs": lax.rem(position + 1, n_pairs)},
        device_id_type=MESH,
    )
    low_copy = pltpu.make_async_remote_copy(
        src_ref=moved.at[out_low],
        dst_ref=moved.at[2 * half - 1],
        send_sem=pair_sem.at[2],
        recv_sem=pair_sem.at[3],
        device_id={"pairs": lax.rem(position + n_pairs - 1, n_pairs)},
        device_id_type=MESH,
    )

    first_turn(half - 1, up_last, 2 * half - 2)

    @pl.when(position < n_pairs - 1)
    def _():
        up_copy.start()

    first_turn(0, not_first, low_zero)

    @pl.when(position > 0)
    def _():
        low_copy.start()

    @pl.loop(1, half - 1)
    def _(k):
        first_turn(k, k + 1, half + k - 1)

    def second_products(k):
        products(
            moved.at[k], moved.at[half + k], later, turned.at[k], rows, partial.at[1, k]
        )

    @pl.loop(1, near - 1)
    def _(at):
        @pl.loop(at * share, (at + 1) * share)
        def _(k):
            second_products(k)

        give(1, at)

    @pl.loop(1, share)
    def _(k):
        second_products(k)

    @pl.loop(half - share, half - 1)
    def _(k):
        second_products(k)

    @pl.when(position > 0)
    def _():
        up_copy.wait_recv()

    second_products(0)
    give(1, 0)

    @pl.when(position < n_pairs - 1)
    def _():
        low_copy.wait_recv()

    second_products(half - 1)
    give(1, near - 1)
    all_coefs(1, later)

    @pl.loop(0, half)
    def _(k):
        rotate(
            moved.at[k], column_block(rotated, k), column_block(rotated, half + k),
            coefs.at[1, k], later[3], turned.at[k], rows,
        )
        tile = coefs[1, k] * (1.0 / (rows * n))
        power[pl.ds(k, 1), :] = tile[6:7, :]
        power[pl.ds(half + k, 1), :] = tile[7:8, :]

    @pl.when(position > 0)
    def _():
        low_copy.wait_send()

    @pl.when(position < n_pairs - 1)
    def _():
        up_copy.wait_send()

    for step in range(STEPS):
        wait_bytes(near_parts.at[step, pl.ds(0, near - 1)], give_sem.at[step])
        wait_bytes(far_parts.at[step, pl.ds(0, far - 1)], pass_sem.at[step])
        wait_bytes(coefs.at[step, pl.ds(0, (near - 1) * share)], spread_sem.at[step])


def per_device(n, n_pairs, loads, col_weights, partner_offsets, skip_mask):
    rows, columns = loads.shape
    half = columns // (2 * BLOCK)
    near = inner_size(half)
    tiles = (TILE, BLOCK)
    vmem = pl.BlockSpec(memory_space=pltpu.VMEM)
    smem = pl.BlockSpec(memory_space=pltpu.SMEM)
    dma = pltpu.SemaphoreType.DMA
    weighted = loads * col_weights[None, :]
    rotated, power = pl.pallas_call(
        functools.partial(turning_kernel, n, n_pairs, half, rows),
        out_shape=(
            jax.ShapeDtypeStruct(loads.shape, jnp.float32),
            jax.ShapeDtypeStruct((2 * half, BLOCK), jnp.float32),
        ),
        in_specs=[vmem, smem, smem],
        out_specs=(vmem, vmem),
        scratch_shapes=[
            pltpu.VMEM((2 * half + 2, rows, BLOCK), jnp.float32),
            pltpu.VMEM((STEPS, half) + tiles, jnp.float32),
            pltpu.VMEM((STEPS, near, half // near) + tiles, jnp.float32),
            pltpu.VMEM((STEPS, n // near, half // near) + tiles, jnp.float32),
            pltpu.VMEM((STEPS, half) + tiles, jnp.float32),
            pltpu.VMEM((half, 3, rows, BLOCK), jnp.float32),
            dma((STEPS,)),
            dma((STEPS,)),
            dma((STEPS,)),
            dma((STEPS,)),
            dma((STEPS,)),
            dma((STEPS,)),
            dma((4,)),
        ],
        compiler_params=pltpu.CompilerParams(
            collective_id=0, has_side_effects=True, vmem_limit_bytes=24 * 1024 * 1024
        ),
        cost_estimate=pl.CostEstimate(
            flops=60 * loads.size, bytes_accessed=8 * loads.size, transcendentals=0
        ),
    )(weighted, partner_offsets, skip_mask)
    return rotated, power.reshape(columns)


def solution(mesh):
    in_specs = (P("rows", "pairs"), P("pairs"), P(), P(None, "pairs"))
    out_specs = (P("rows", "pairs"), P("pairs"))
    return jax.shard_map(
        functools.partial(per_device, mesh.shape["rows"], mesh.shape["pairs"]),
        mesh=mesh, in_specs=in_specs, out_specs=out_specs, check_vma=False,
    )
```

```python
import functools
import jax
import jax.numpy as jnp
from jax import lax
from jax.experimental import pallas as pl
from jax.experimental.pallas import tpu as pltpu
from jax.sharding import PartitionSpec as P

BLOCK = 128
STEPS = 2
TILE = 8
CHUNK = 32
MESH = pl.DeviceIdType.MESH


def rolled(x, shift):
    return pltpu.roll(x, shift, 1)


def fold(x):
    return jnp.sum(x.reshape(x.shape[0] // TILE, TILE, BLOCK), axis=0)


def shifts_of(offsets, step):
    first, second = offsets[step, 0], offsets[step, 1]
    to_first = lax.rem(BLOCK - first, BLOCK)
    to_second = lax.rem(BLOCK - second, BLOCK)
    between = lax.rem(BLOCK + first - second, BLOCK)
    return to_first, to_second, between, second


def chunks(rows, body, carry):
    def step(at, carry):
        return body(pl.ds(pl.multiple_of(at * CHUNK, CHUNK), CHUNK), carry)

    return lax.fori_loop(0, rows // CHUNK, step, carry, unroll=True)


def products(upper, lower, shifts, turned, rows, partial):
    to_first, to_second, between, _ = shifts

    def body(spot, sums):
        u, l = upper[spot, :], lower[spot, :]
        lp, ud, ld = rolled(l, to_first), rolled(u, between), rolled(l, to_second)
        for at, x in enumerate((lp, ud, ld)):
            turned[at, spot, :] = x
        pairs = ((u, u), (l, l), (u, lp), (u, ud), (u, ld), (lp, ud), (lp, ld))
        return tuple(total + fold(a * b) for total, (a, b) in zip(sums, pairs))

    zero = jnp.zeros((TILE, BLOCK), jnp.float32)
    sums = chunks(rows, body, (zero,) * 7)
    for at, total in enumerate(sums):
        partial[pl.ds(at, 1), :] = jnp.sum(total, axis=0, keepdims=True)
    partial[pl.ds(7, 1), :] = jnp.zeros((1, BLOCK), jnp.float32)


def angle(a, b, g):
    half_gap = 0.5 * (b - a)
    sign = jnp.where(half_gap >= 0.0, 1.0, -1.0)
    denominator = jnp.maximum(
        jnp.abs(half_gap) + jnp.sqrt(half_gap * half_gap + g * g), 1e-06 * (a + b)
    )
    t = sign * g / denominator
    c = 1.0 / jnp.sqrt(1.0 + t * t)
    return c, t * c


def norms(a, b, g, c, s):
    cross = 2.0 * c * s * g
    return c * c * a - cross + s * s * b, s * s * a + cross + c * c * b


def turn(total, skip, shifts):
    to_first, _, between, back = shifts
    row = [jnp.broadcast_to(total[at : at + 1, :], (TILE, BLOCK)) for at in range(7)]
    a, b, g, u_ud, u_ld, l_ud, l_ld = row
    b = rolled(b, to_first)
    keep = jnp.full((TILE, BLOCK), skip, jnp.int32) == 0
    c, s = angle(a, b, g)
    c, s = jnp.where(keep, c, 1.0), jnp.where(keep, s, 0.0)
    a1, b1 = norms(a, b, g, c, s)
    cd, sd, bd = rolled(c, between), rolled(s, between), rolled(b1, between)
    g1 = c * (sd * u_ud + cd * u_ld) - s * (sd * l_ud + cd * l_ld)
    c2, s2 = angle(a1, bd, g1)
    c2, s2 = jnp.where(keep, c2, 1.0), jnp.where(keep, s2, 0.0)
    a2, b2 = norms(a1, bd, g1, c2, s2)
    place = lax.broadcasted_iota(jnp.int32, (TILE, BLOCK), 0)
    tile = rolled(b2, back)
    for at, value in enumerate((c, s, cd, sd, c2, s2, a2)):
        tile = jnp.where(place == at, value, tile)
    return tile


def factors(coefs):
    tile = coefs[...]
    c, s, cd, sd, c2, s2 = (
        jnp.broadcast_to(tile[at : at + 1, :], (TILE, BLOCK)) for at in range(6)
    )
    up = (c2 * c, -c2 * s, -s2 * sd, -s2 * cd)
    low = (s2 * c, -s2 * s, c2 * sd, c2 * cd)
    return up, low


def mix(weights, parts):
    shape = (CHUNK // TILE, TILE, BLOCK)
    total = sum(w[None] * x.reshape(shape) for w, x in zip(weights, parts))
    return total.reshape(CHUNK, BLOCK)


def rotate(upper, new_upper, new_lower, coefs, back, turned, rows):
    up, low = factors(coefs)

    def body(spot, carry):
        parts = [upper[spot, :]] + [turned[at, spot, :] for at in range(3)]
        new_upper[spot, :] = mix(up, parts)
        new_lower[spot, :] = rolled(mix(low, parts), back)
        return carry

    chunks(rows, body, 0)


def rotate_one(pair, new, coefs, shifts, rows, which):
    weights = factors(coefs)[which]
    to_first, to_second, between, back = shifts

    def body(spot, carry):
        u, l = pair[0, spot, :], pair[1, spot, :]
        parts = (u, rolled(l, to_first), rolled(u, between), rolled(l, to_second))
        x = mix(weights, parts)
        new[spot, :] = rolled(x, back) if which else x
        return carry

    chunks(rows, body, 0)


def column_block(array, block):
    return array.at[:, pl.ds(pl.multiple_of(block * BLOCK, BLOCK), BLOCK)]


def turning_kernel(
    n, n_pairs, half, rows,
    data, offsets, skips,
    rotated, power,
    moved, partial, arrived, coefs, turned, guests, guest_coefs,
    give_sem, arrive_sem, spread_sem, coef_sem, guest_sem, guest_coef_sem,
):
    me, position = lax.axis_index("rows"), lax.axis_index("pairs")
    copies = n // half
    own, group = me // copies, lax.rem(me, copies)
    not_first = (position + n_pairs - 1) // n_pairs
    is_last = (position + 1) // n_pairs

    barrier = pltpu.get_barrier_semaphore()

    @pl.loop(1, n)
    def _(by):
        pl.semaphore_signal(
            barrier, inc=1, device_id={"rows": lax.rem(me + by, n)}, device_id_type=MESH
        )

    def greet_pairs(to):
        pl.semaphore_signal(barrier, inc=1, device_id={"pairs": to}, device_id_type=MESH)

        @pl.loop(0, half)
        def _(at):
            pl.semaphore_signal(
                barrier, inc=1,
                device_id={"rows": at * copies + group, "pairs": to}, device_id_type=MESH,
            )

    @pl.when(position > 0)
    def _():
        greet_pairs(position - 1)

    @pl.when(position < n_pairs - 1)
    def _():
        greet_pairs(position + 1)

    def give(step, k):
        @pl.loop(0, copies)
        def _(at):
            to = k * copies + at

            @pl.when(to != me)
            def _():
                pltpu.make_async_remote_copy(
                    src_ref=partial.at[step, k],
                    dst_ref=arrived.at[step, me],
                    send_sem=give_sem.at[step],
                    recv_sem=arrive_sem.at[step],
                    device_id={"rows": to},
                    device_id_type=MESH,
                ).start()

            @pl.when(to == me)
            def _():
                arrived[step, me] = partial[step, k]

    def own_coefs(step, shifts):
        some = arrived.at[step, pl.ds(0, n - 1)]
        pltpu.make_async_copy(some, some, arrive_sem.at[step]).wait()
        total = jnp.sum(arrived[step], axis=0)
        coefs[step, own] = turn(total, skips[step, own], shifts)

        @pl.loop(1, half)
        def _(by):
            to = lax.rem(own + by, half) * copies + group
            pltpu.make_async_remote_copy(
                src_ref=coefs.at[step, own],
                dst_ref=coefs.at[step, own],
                send_sem=spread_sem.at[step],
                recv_sem=coef_sem.at[step, own],
                device_id={"rows": to},
                device_id_type=MESH,
            ).start()

    has_next, has_last = position < n_pairs - 1, position > 0
    after, before = lax.rem(position + 1, n_pairs), lax.rem(position + n_pairs - 1, n_pairs)

    def lend(k, side, to):
        for at, block in enumerate((k, half + k)):
            pltpu.make_async_remote_copy(
                src_ref=column_block(data, block),
                dst_ref=guests.at[side, at],
                send_sem=guest_sem.at[side, 0],
                recv_sem=guest_sem.at[side, 1],
                device_id={"pairs": to},
                device_id_type=MESH,
            ).start()

    def lend_coefs(k, side, to):
        @pl.loop(0, half)
        def _(at):
            pltpu.make_async_remote_copy(
                src_ref=coefs.at[0, k],
                dst_ref=guest_coefs.at[side],
                send_sem=guest_coef_sem.at[side, 0],
                recv_sem=guest_coef_sem.at[side, 1],
                device_id={"rows": at * copies + group, "pairs": to},
                device_id_type=MESH,
            ).start()

    def wait_bytes(ref, sem):
        pltpu.make_async_copy(ref, ref, sem).wait()

    def wait_guest(side):
        wait_bytes(guests.at[side], guest_sem.at[side, 1])
        wait_bytes(guest_coefs.at[side], guest_coef_sem.at[side, 1])

    def wait_coefs(step, k):
        tile = coefs.at[step, k]

        @pl.when(k != own)
        def _():
            pltpu.make_async_copy(tile, tile, coef_sem.at[step, k]).wait()

    shifts, later = shifts_of(offsets, 0), shifts_of(offsets, 1)

    def first_products(k):
        products(
            column_block(data, k), column_block(data, half + k), shifts, turned.at[k],
            rows, partial.at[0, k],
        )

    early = half // 2

    @pl.loop(0, early)
    def _(k):
        first_products(k)

    pl.semaphore_wait(barrier, n - 1 + (1 + half) * (not_first + 1 - is_last))

    @pl.when(has_next)
    def _():
        lend(half - 1, 0, after)

    @pl.when(has_last)
    def _():
        lend(0, 1, before)


    @pl.loop(0, early)
    def _(k):
        give(0, k)

    @pl.loop(early, half)
    def _(k):
        first_products(k)
        give(0, k)

    own_coefs(0, shifts)

    @pl.when(has_next & (own == half - 1))
    def _():
        lend_coefs(half - 1, 0, after)

    @pl.when(has_last & (own == 0))
    def _():
        lend_coefs(0, 1, before)

    def first_turn(k, upper_to, lower_to):
        wait_coefs(0, k)
        rotate(
            column_block(data, k), moved.at[upper_to], moved.at[lower_to],
            coefs.at[0, k], shifts[3], turned.at[k], rows,
        )

    out_low, out_up = 2 * half, 2 * half + 1
    low_zero = (1 - not_first) + out_low * not_first
    up_last = (2 * half - 1) * is_last + out_up * (1 - is_last)
    first_turn(half - 1, up_last, 2 * half - 2)
    first_turn(0, not_first, low_zero)

    @pl.loop(1, half - 1)
    def _(k):
        first_turn(k, k + 1, half + k - 1)

    def second_products(k):
        products(
            moved.at[k], moved.at[half + k], later, turned.at[k], rows, partial.at[1, k]
        )
        give(1, k)

    @pl.loop(1, half - 1)
    def _(k):
        second_products(k)

    @pl.when(position > 0)
    def _():
        wait_guest(0)
        rotate_one(guests.at[0], moved.at[0], guest_coefs.at[0], shifts, rows, 0)

    second_products(0)

    @pl.when(position < n_pairs - 1)
    def _():
        wait_guest(1)
        rotate_one(guests.at[1], moved.at[2 * half - 1], guest_coefs.at[1], shifts, rows, 1)

    second_products(half - 1)
    own_coefs(1, later)

    @pl.loop(0, half)
    def _(k):
        wait_coefs(1, k)
        rotate(
            moved.at[k], column_block(rotated, k), column_block(rotated, half + k),
            coefs.at[1, k], later[3], turned.at[k], rows,
        )
        tile = coefs[1, k] * (1.0 / (rows * n))
        power[pl.ds(k, 1), :] = tile[6:7, :]
        power[pl.ds(half + k, 1), :] = tile[7:8, :]

    for side, lent, lender in ((0, has_next, half - 1), (1, has_last, 0)):

        @pl.when(lent)
        def _():
            wait_bytes(guests.at[side], guest_sem.at[side, 0])

        @pl.when(lent & (own == lender))
        def _():
            wait_bytes(coefs.at[0], guest_coef_sem.at[side, 0])

    for step in range(STEPS):
        some = arrived.at[step, pl.ds(0, n - 1)]
        pltpu.make_async_copy(some, some, give_sem.at[step]).wait()
        rest = coefs.at[step, pl.ds(0, half - 1)]
        pltpu.make_async_copy(rest, rest, spread_sem.at[step]).wait()


def per_device(n, n_pairs, loads, col_weights, partner_offsets, skip_mask):
    rows, columns = loads.shape
    half = columns // (2 * BLOCK)
    tiles = (TILE, BLOCK)
    vmem = pl.BlockSpec(memory_space=pltpu.VMEM)
    smem = pl.BlockSpec(memory_space=pltpu.SMEM)
    dma = pltpu.SemaphoreType.DMA
    weighted = loads * col_weights[None, :]
    rotated, power = pl.pallas_call(
        functools.partial(turning_kernel, n, n_pairs, half, rows),
        out_shape=(
            jax.ShapeDtypeStruct(loads.shape, jnp.float32),
            jax.ShapeDtypeStruct((2 * half, BLOCK), jnp.float32),
        ),
        in_specs=[vmem, smem, smem],
        out_specs=(vmem, vmem),
        scratch_shapes=[
            pltpu.VMEM((2 * half + 2, rows, BLOCK), jnp.float32),
            pltpu.VMEM((STEPS, half) + tiles, jnp.float32),
            pltpu.VMEM((STEPS, n) + tiles, jnp.float32),
            pltpu.VMEM((STEPS, half) + tiles, jnp.float32),
            pltpu.VMEM((half, 3, rows, BLOCK), jnp.float32),
            pltpu.VMEM((2, 2, rows, BLOCK), jnp.float32),
            pltpu.VMEM((2,) + tiles, jnp.float32),
            dma((STEPS,)),
            dma((STEPS,)),
            dma((STEPS,)),
            dma((STEPS, half)),
            dma((2, 2)),
            dma((2, 2)),
        ],
        compiler_params=pltpu.CompilerParams(
            collective_id=0, has_side_effects=True, vmem_limit_bytes=24 * 1024 * 1024
        ),
        cost_estimate=pl.CostEstimate(
            flops=60 * loads.size, bytes_accessed=8 * loads.size, transcendentals=0
        ),
    )(weighted, partner_offsets, skip_mask)
    return rotated, power.reshape(columns)


def solution(mesh):
    in_specs = (P("rows", "pairs"), P("pairs"), P(), P(None, "pairs"))
    out_specs = (P("rows", "pairs"), P("pairs"))
    return jax.shard_map(
        functools.partial(per_device, mesh.shape["rows"], mesh.shape["pairs"]),
        mesh=mesh, in_specs=in_specs, out_specs=out_specs, check_vma=False,
    )
```

```python
import functools
import jax
import jax.numpy as jnp
from jax import lax
from jax.experimental import pallas as pl
from jax.experimental.pallas import tpu as pltpu
from jax.sharding import PartitionSpec as P

BLOCK = 128
STEPS = 2
TILE = 8
CHUNK = 32
DEPTH = 2
MESH = pl.DeviceIdType.MESH


def rolled(x, shift):
    return pltpu.roll(x, shift, 1)


def fold(x):
    return jnp.sum(x.reshape(x.shape[0] // TILE, TILE, BLOCK), axis=0)


def shifts_of(offsets, step):
    first, second = offsets[step, 0], offsets[step, 1]
    to_first = lax.rem(BLOCK - first, BLOCK)
    to_second = lax.rem(BLOCK - second, BLOCK)
    between = lax.rem(BLOCK + first - second, BLOCK)
    return to_first, to_second, between, second


def spots(rows):
    return [pl.ds(at * CHUNK, CHUNK) for at in range(rows // CHUNK)]


class Later:
    def __init__(self):
        self.waiting = []

    def add(self, stores):
        self.waiting.append(stores)
        if len(self.waiting) > DEPTH:
            self.write(self.waiting.pop(0))

    def write(self, stores):
        for ref, index, value in stores:
            ref[index] = value

    def end(self):
        for stores in self.waiting:
            self.write(stores)


def products(pairs, shifts, rows):
    to_first, to_second, between, _ = shifts
    later = Later()
    for upper, lower, turned, partial in pairs:
        sums = [jnp.zeros((TILE, BLOCK), jnp.float32)] * 7
        for spot in spots(rows):
            u, l = upper[spot, :], lower[spot, :]
            lp, ud, ld = rolled(l, to_first), rolled(u, between), rolled(l, to_second)
            factor_pairs = ((u, u), (l, l), (u, lp), (u, ud), (u, ld), (lp, ud), (lp, ld))
            sums = [total + fold(a * b) for total, (a, b) in zip(sums, factor_pairs)]
            later.add([(turned, (at, spot), x) for at, x in enumerate((lp, ud, ld))])
        ends = [jnp.sum(total, axis=0, keepdims=True) for total in sums]
        ends.append(jnp.zeros((1, BLOCK), jnp.float32))
        later.add([(partial, pl.ds(at, 1), x) for at, x in enumerate(ends)])
    later.end()


def angle(a, b, g):
    half_gap = 0.5 * (b - a)
    sign = jnp.where(half_gap >= 0.0, 1.0, -1.0)
    denominator = jnp.maximum(
        jnp.abs(half_gap) + jnp.sqrt(half_gap * half_gap + g * g), 1e-06 * (a + b)
    )
    t = sign * g / denominator
    c = 1.0 / jnp.sqrt(1.0 + t * t)
    return c, t * c


def norms(a, b, g, c, s):
    cross = 2.0 * c * s * g
    return c * c * a - cross + s * s * b, s * s * a + cross + c * c * b


def turn(total, skip, shifts):
    to_first, _, between, back = shifts
    row = [jnp.broadcast_to(total[at : at + 1, :], (TILE, BLOCK)) for at in range(7)]
    a, b, g, u_ud, u_ld, l_ud, l_ld = row
    b = rolled(b, to_first)
    keep = jnp.full((TILE, BLOCK), skip, jnp.int32) == 0
    c, s = angle(a, b, g)
    c, s = jnp.where(keep, c, 1.0), jnp.where(keep, s, 0.0)
    a1, b1 = norms(a, b, g, c, s)
    cd, sd, bd = rolled(c, between), rolled(s, between), rolled(b1, between)
    g1 = c * (sd * u_ud + cd * u_ld) - s * (sd * l_ud + cd * l_ld)
    c2, s2 = angle(a1, bd, g1)
    c2, s2 = jnp.where(keep, c2, 1.0), jnp.where(keep, s2, 0.0)
    a2, b2 = norms(a1, bd, g1, c2, s2)
    place = lax.broadcasted_iota(jnp.int32, (TILE, BLOCK), 0)
    tile = rolled(b2, back)
    for at, value in enumerate((c, s, cd, sd, c2, s2, a2)):
        tile = jnp.where(place == at, value, tile)
    return tile


def factors(coefs):
    tile = coefs[...]
    c, s, cd, sd, c2, s2 = (
        jnp.broadcast_to(tile[at : at + 1, :], (TILE, BLOCK)) for at in range(6)
    )
    up = (c2 * c, -c2 * s, -s2 * sd, -s2 * cd)
    low = (s2 * c, -s2 * s, c2 * sd, c2 * cd)
    return up, low


def mix(weights, parts):
    shape = (CHUNK // TILE, TILE, BLOCK)
    total = sum(w[None] * x.reshape(shape) for w, x in zip(weights, parts))
    return total.reshape(CHUNK, BLOCK)


def rotate(pairs, back, rows):
    later = Later()
    weights = [factors(pair[3]) for pair in pairs]
    for (upper, new_upper, new_lower, _, turned), (up, low) in zip(pairs, weights):
        for spot in spots(rows):
            parts = [upper[spot, :]] + [turned[at, spot, :] for at in range(3)]
            low_part = rolled(mix(low, parts), back)
            later.add([(new_upper, spot, mix(up, parts)), (new_lower, spot, low_part)])
    later.end()


def rotate_one(pair, new, coefs, shifts, rows, which):
    weights = factors(coefs)[which]
    to_first, to_second, between, back = shifts
    later = Later()
    for spot in spots(rows):
        u, l = pair[0, spot, :], pair[1, spot, :]
        parts = (u, rolled(l, to_first), rolled(u, between), rolled(l, to_second))
        x = mix(weights, parts)
        later.add([(new, spot, rolled(x, back) if which else x)])
    later.end()


def column_block(array, block):
    return array.at[:, pl.ds(pl.multiple_of(block * BLOCK, BLOCK), BLOCK)]


def turning_kernel(
    n, n_pairs, half, rows,
    data, offsets, skips,
    rotated, power,
    moved, partial, arrived, coefs, turned, guests, guest_coefs,
    give_sem, arrive_sem, spread_sem, coef_sem, guest_sem, guest_coef_sem,
):
    me, position = lax.axis_index("rows"), lax.axis_index("pairs")
    copies = n // half
    own, group = me // copies, lax.rem(me, copies)
    not_first = (position + n_pairs - 1) // n_pairs
    is_last = (position + 1) // n_pairs

    barrier = pltpu.get_barrier_semaphore()

    @pl.loop(1, n)
    def _(by):
        pl.semaphore_signal(
            barrier, inc=1, device_id={"rows": lax.rem(me + by, n)}, device_id_type=MESH
        )

    def greet_pairs(to):
        pl.semaphore_signal(barrier, inc=1, device_id={"pairs": to}, device_id_type=MESH)

        @pl.loop(0, half)
        def _(at):
            pl.semaphore_signal(
                barrier, inc=1,
                device_id={"rows": at * copies + group, "pairs": to}, device_id_type=MESH,
            )

    @pl.when(position > 0)
    def _():
        greet_pairs(position - 1)

    @pl.when(position < n_pairs - 1)
    def _():
        greet_pairs(position + 1)

    def give(step, k):
        @pl.loop(0, copies)
        def _(at):
            to = k * copies + at

            @pl.when(to != me)
            def _():
                pltpu.make_async_remote_copy(
                    src_ref=partial.at[step, k],
                    dst_ref=arrived.at[step, me],
                    send_sem=give_sem.at[step],
                    recv_sem=arrive_sem.at[step],
                    device_id={"rows": to},
                    device_id_type=MESH,
                ).start()

            @pl.when(to == me)
            def _():
                arrived[step, me] = partial[step, k]

    def own_coefs(step, shifts):
        some = arrived.at[step, pl.ds(0, n - 1)]
        pltpu.make_async_copy(some, some, arrive_sem.at[step]).wait()
        total = jnp.sum(arrived[step], axis=0)
        coefs[step, own] = turn(total, skips[step, own], shifts)

        @pl.loop(1, half)
        def _(by):
            to = lax.rem(own + by, half) * copies + group
            pltpu.make_async_remote_copy(
                src_ref=coefs.at[step, own],
                dst_ref=coefs.at[step, own],
                send_sem=spread_sem.at[step],
                recv_sem=coef_sem.at[step, own],
                device_id={"rows": to},
                device_id_type=MESH,
            ).start()

    has_next, has_last = position < n_pairs - 1, position > 0
    after, before = lax.rem(position + 1, n_pairs), lax.rem(position + n_pairs - 1, n_pairs)

    def lend(k, side, to):
        for at, block in enumerate((k, half + k)):
            pltpu.make_async_remote_copy(
                src_ref=column_block(data, block),
                dst_ref=guests.at[side, at],
                send_sem=guest_sem.at[side, 0],
                recv_sem=guest_sem.at[side, 1],
                device_id={"pairs": to},
                device_id_type=MESH,
            ).start()

    def lend_coefs(k, side, to):
        @pl.loop(0, half)
        def _(at):
            pltpu.make_async_remote_copy(
                src_ref=coefs.at[0, k],
                dst_ref=guest_coefs.at[side],
                send_sem=guest_coef_sem.at[side, 0],
                recv_sem=guest_coef_sem.at[side, 1],
                device_id={"rows": at * copies + group, "pairs": to},
                device_id_type=MESH,
            ).start()

    def wait_bytes(ref, sem):
        pltpu.make_async_copy(ref, ref, sem).wait()

    def wait_guest(side):
        wait_bytes(guests.at[side], guest_sem.at[side, 1])
        wait_bytes(guest_coefs.at[side], guest_coef_sem.at[side, 1])

    def wait_coefs(step, k):
        tile = coefs.at[step, k]

        @pl.when(k != own)
        def _():
            pltpu.make_async_copy(tile, tile, coef_sem.at[step, k]).wait()

    shifts, later = shifts_of(offsets, 0), shifts_of(offsets, 1)

    def first_pair(k):
        upper, lower = column_block(data, k), column_block(data, half + k)
        return upper, lower, turned.at[k], partial.at[0, k]

    def second_pair(k):
        return moved.at[k], moved.at[half + k], turned.at[k], partial.at[1, k]

    early = half // 4

    @pl.loop(0, early)
    def _(at):
        products([first_pair(2 * at), first_pair(2 * at + 1)], shifts, rows)

    pl.semaphore_wait(barrier, n - 1 + (1 + half) * (not_first + 1 - is_last))

    @pl.when(has_next)
    def _():
        lend(half - 1, 0, after)

    @pl.when(has_last)
    def _():
        lend(0, 1, before)


    @pl.loop(0, 2 * early)
    def _(k):
        give(0, k)

    @pl.loop(early, half // 2)
    def _(at):
        products([first_pair(2 * at), first_pair(2 * at + 1)], shifts, rows)
        give(0, 2 * at)
        give(0, 2 * at + 1)

    own_coefs(0, shifts)

    @pl.when(has_next & (own == half - 1))
    def _():
        lend_coefs(half - 1, 0, after)

    @pl.when(has_last & (own == 0))
    def _():
        lend_coefs(0, 1, before)

    def first_turn(k, upper_to, lower_to):
        upper = column_block(data, k)
        return upper, moved.at[upper_to], moved.at[lower_to], coefs.at[0, k], turned.at[k]

    def last_turn(k):
        upper, lower = column_block(rotated, k), column_block(rotated, half + k)
        return moved.at[k], upper, lower, coefs.at[1, k], turned.at[k]

    out_low, out_up = 2 * half, 2 * half + 1
    low_zero = (1 - not_first) + out_low * not_first
    up_last = (2 * half - 1) * is_last + out_up * (1 - is_last)
    wait_coefs(0, half - 1)
    wait_coefs(0, 0)
    ends = [first_turn(half - 1, up_last, 2 * half - 2), first_turn(0, not_first, low_zero)]
    rotate(ends, shifts[3], rows)

    @pl.loop(0, half // 2 - 1)
    def _(at):
        inner = (2 * at + 1, 2 * at + 2)
        for k in inner:
            wait_coefs(0, k)
        rotate([first_turn(k, k + 1, half + k - 1) for k in inner], shifts[3], rows)

    @pl.loop(0, half // 2 - 1)
    def _(at):
        inner = (2 * at + 1, 2 * at + 2)
        products([second_pair(k) for k in inner], later, rows)
        for k in inner:
            give(1, k)

    @pl.when(position > 0)
    def _():
        wait_guest(0)
        rotate_one(guests.at[0], moved.at[0], guest_coefs.at[0], shifts, rows, 0)

    @pl.when(position < n_pairs - 1)
    def _():
        wait_guest(1)
        rotate_one(guests.at[1], moved.at[2 * half - 1], guest_coefs.at[1], shifts, rows, 1)

    products([second_pair(0), second_pair(half - 1)], later, rows)
    give(1, 0)
    give(1, half - 1)
    own_coefs(1, later)

    @pl.loop(0, half // 2)
    def _(at):
        two = (2 * at, 2 * at + 1)
        for k in two:
            wait_coefs(1, k)
        rotate([last_turn(k) for k in two], later[3], rows)
        for k in two:
            tile = coefs[1, k] * (1.0 / (rows * n))
            power[pl.ds(k, 1), :] = tile[6:7, :]
            power[pl.ds(half + k, 1), :] = tile[7:8, :]

    for side, lent, lender in ((0, has_next, half - 1), (1, has_last, 0)):

        @pl.when(lent)
        def _():
            wait_bytes(guests.at[side], guest_sem.at[side, 0])

        @pl.when(lent & (own == lender))
        def _():
            wait_bytes(coefs.at[0], guest_coef_sem.at[side, 0])

    for step in range(STEPS):
        some = arrived.at[step, pl.ds(0, n - 1)]
        pltpu.make_async_copy(some, some, give_sem.at[step]).wait()
        rest = coefs.at[step, pl.ds(0, half - 1)]
        pltpu.make_async_copy(rest, rest, spread_sem.at[step]).wait()


def per_device(n, n_pairs, loads, col_weights, partner_offsets, skip_mask):
    rows, columns = loads.shape
    half = columns // (2 * BLOCK)
    tiles = (TILE, BLOCK)
    vmem = pl.BlockSpec(memory_space=pltpu.VMEM)
    smem = pl.BlockSpec(memory_space=pltpu.SMEM)
    dma = pltpu.SemaphoreType.DMA
    weighted = loads * col_weights[None, :]
    rotated, power = pl.pallas_call(
        functools.partial(turning_kernel, n, n_pairs, half, rows),
        out_shape=(
            jax.ShapeDtypeStruct(loads.shape, jnp.float32),
            jax.ShapeDtypeStruct((2 * half, BLOCK), jnp.float32),
        ),
        in_specs=[vmem, smem, smem],
        out_specs=(vmem, vmem),
        scratch_shapes=[
            pltpu.VMEM((2 * half + 2, rows, BLOCK), jnp.float32),
            pltpu.VMEM((STEPS, half) + tiles, jnp.float32),
            pltpu.VMEM((STEPS, n) + tiles, jnp.float32),
            pltpu.VMEM((STEPS, half) + tiles, jnp.float32),
            pltpu.VMEM((half, 3, rows, BLOCK), jnp.float32),
            pltpu.VMEM((2, 2, rows, BLOCK), jnp.float32),
            pltpu.VMEM((2,) + tiles, jnp.float32),
            dma((STEPS,)),
            dma((STEPS,)),
            dma((STEPS,)),
            dma((STEPS, half)),
            dma((2, 2)),
            dma((2, 2)),
        ],
        compiler_params=pltpu.CompilerParams(
            collective_id=0, has_side_effects=True, vmem_limit_bytes=24 * 1024 * 1024
        ),
        cost_estimate=pl.CostEstimate(
            flops=60 * loads.size, bytes_accessed=8 * loads.size, transcendentals=0
        ),
    )(weighted, partner_offsets, skip_mask)
    return rotated, power.reshape(columns)


def solution(mesh):
    in_specs = (P("rows", "pairs"), P("pairs"), P(), P(None, "pairs"))
    out_specs = (P("rows", "pairs"), P("pairs"))
    return jax.shard_map(
        functools.partial(per_device, mesh.shape["rows"], mesh.shape["pairs"]),
        mesh=mesh, in_specs=in_specs, out_specs=out_specs, check_vma=False,
    )
```

```python
import functools
import jax
import jax.numpy as jnp
from jax import lax
from jax.experimental import pallas as pl
from jax.experimental.pallas import tpu as pltpu
from jax.sharding import PartitionSpec as P

BLOCK = 128
STEPS = 2
TILE = 8
CHUNK = 32
DEPTH = 2
MESH = pl.DeviceIdType.MESH


def rolled(x, shift):
    return pltpu.roll(x, shift, 1)


def fold(x):
    return jnp.sum(x.reshape(x.shape[0] // TILE, TILE, BLOCK), axis=0)


def shifts_of(offsets, step):
    first, second = offsets[step, 0], offsets[step, 1]
    to_first = lax.rem(BLOCK - first, BLOCK)
    to_second = lax.rem(BLOCK - second, BLOCK)
    between = lax.rem(BLOCK + first - second, BLOCK)
    return to_first, to_second, between, second


def spots(rows):
    return [pl.ds(at * CHUNK, CHUNK) for at in range(rows // CHUNK)]


class Later:
    def __init__(self):
        self.waiting = []

    def add(self, stores):
        self.waiting.append(stores)
        if len(self.waiting) > DEPTH:
            self.write(self.waiting.pop(0))

    def write(self, stores):
        for ref, index, value in stores:
            ref[index] = value

    def end(self):
        for stores in self.waiting:
            self.write(stores)


def products(pairs, shifts, rows):
    to_first, to_second, between, _ = shifts
    later = Later()
    for upper, lower, turned, partial in pairs:
        sums = [jnp.zeros((TILE, BLOCK), jnp.float32)] * 7
        for spot in spots(rows):
            u, l = upper[spot, :], lower[spot, :]
            lp, ud, ld = rolled(l, to_first), rolled(u, between), rolled(l, to_second)
            factor_pairs = ((u, u), (l, l), (u, lp), (u, ud), (u, ld), (lp, ud), (lp, ld))
            sums = [total + fold(a * b) for total, (a, b) in zip(sums, factor_pairs)]
            later.add([(turned, (at, spot), x) for at, x in enumerate((lp, ud, ld))])
        ends = [jnp.sum(total, axis=0, keepdims=True) for total in sums]
        ends.append(jnp.zeros((1, BLOCK), jnp.float32))
        later.add([(partial, pl.ds(at, 1), x) for at, x in enumerate(ends)])
    later.end()


def angle(a, b, g):
    half_gap = 0.5 * (b - a)
    sign = jnp.where(half_gap >= 0.0, 1.0, -1.0)
    denominator = jnp.maximum(
        jnp.abs(half_gap) + jnp.sqrt(half_gap * half_gap + g * g), 1e-06 * (a + b)
    )
    t = sign * g / denominator
    c = 1.0 / jnp.sqrt(1.0 + t * t)
    return c, t * c


def norms(a, b, g, c, s):
    cross = 2.0 * c * s * g
    return c * c * a - cross + s * s * b, s * s * a + cross + c * c * b


def turn(total, skip, shifts):
    to_first, _, between, back = shifts
    row = [jnp.broadcast_to(total[at : at + 1, :], (TILE, BLOCK)) for at in range(7)]
    a, b, g, u_ud, u_ld, l_ud, l_ld = row
    b = rolled(b, to_first)
    keep = jnp.full((TILE, BLOCK), skip, jnp.int32) == 0
    c, s = angle(a, b, g)
    c, s = jnp.where(keep, c, 1.0), jnp.where(keep, s, 0.0)
    a1, b1 = norms(a, b, g, c, s)
    cd, sd, bd = rolled(c, between), rolled(s, between), rolled(b1, between)
    g1 = c * (sd * u_ud + cd * u_ld) - s * (sd * l_ud + cd * l_ld)
    c2, s2 = angle(a1, bd, g1)
    c2, s2 = jnp.where(keep, c2, 1.0), jnp.where(keep, s2, 0.0)
    a2, b2 = norms(a1, bd, g1, c2, s2)
    place = lax.broadcasted_iota(jnp.int32, (TILE, BLOCK), 0)
    tile = rolled(b2, back)
    for at, value in enumerate((c, s, cd, sd, c2, s2, a2)):
        tile = jnp.where(place == at, value, tile)
    return tile


def factors(coefs):
    tile = coefs[...]
    c, s, cd, sd, c2, s2 = (
        jnp.broadcast_to(tile[at : at + 1, :], (TILE, BLOCK)) for at in range(6)
    )
    up = (c2 * c, -c2 * s, -s2 * sd, -s2 * cd)
    low = (s2 * c, -s2 * s, c2 * sd, c2 * cd)
    return up, low


def mix(weights, parts):
    shape = (CHUNK // TILE, TILE, BLOCK)
    total = sum(w[None] * x.reshape(shape) for w, x in zip(weights, parts))
    return total.reshape(CHUNK, BLOCK)


def rotate(pairs, back, rows):
    later = Later()
    weights = [factors(pair[3]) for pair in pairs]
    for (upper, new_upper, new_lower, _, turned), (up, low) in zip(pairs, weights):
        for spot in spots(rows):
            parts = [upper[spot, :]] + [turned[at, spot, :] for at in range(3)]
            low_part = rolled(mix(low, parts), back)
            later.add([(new_upper, spot, mix(up, parts)), (new_lower, spot, low_part)])
    later.end()


def rotate_one(pair, new, coefs, shifts, rows, which):
    weights = factors(coefs)[which]
    to_first, to_second, between, back = shifts
    later = Later()
    for spot in spots(rows):
        u, l = pair[0, spot, :], pair[1, spot, :]
        parts = (u, rolled(l, to_first), rolled(u, between), rolled(l, to_second))
        x = mix(weights, parts)
        later.add([(new, spot, rolled(x, back) if which else x)])
    later.end()


def column_block(array, block):
    return array.at[:, pl.ds(pl.multiple_of(block * BLOCK, BLOCK), BLOCK)]


def turning_kernel(
    n, n_pairs, half, rows,
    data, offsets, skips,
    rotated, power,
    moved, partial, arrived, coefs, turned, guests, guest_coefs,
    give_sem, arrive_sem, spread_sem, coef_sem, guest_sem, guest_coef_sem,
):
    me, position = lax.axis_index("rows"), lax.axis_index("pairs")
    copies = n // half
    own, group = me // copies, lax.rem(me, copies)
    not_first = (position + n_pairs - 1) // n_pairs
    is_last = (position + 1) // n_pairs

    barrier = pltpu.get_barrier_semaphore()

    @pl.loop(1, n)
    def _(by):
        pl.semaphore_signal(
            barrier, inc=1, device_id={"rows": lax.rem(me + by, n)}, device_id_type=MESH
        )

    def greet_pairs(to):
        pl.semaphore_signal(barrier, inc=1, device_id={"pairs": to}, device_id_type=MESH)

        @pl.loop(0, half)
        def _(at):
            pl.semaphore_signal(
                barrier, inc=1,
                device_id={"rows": at * copies + group, "pairs": to}, device_id_type=MESH,
            )

    @pl.when(position > 0)
    def _():
        greet_pairs(position - 1)

    @pl.when(position < n_pairs - 1)
    def _():
        greet_pairs(position + 1)

    def give(step, k):
        @pl.loop(0, copies)
        def _(at):
            to = k * copies + at

            @pl.when(to != me)
            def _():
                pltpu.make_async_remote_copy(
                    src_ref=partial.at[step, k],
                    dst_ref=arrived.at[step, me],
                    send_sem=give_sem.at[step],
                    recv_sem=arrive_sem.at[step],
                    device_id={"rows": to},
                    device_id_type=MESH,
                ).start()

            @pl.when(to == me)
            def _():
                arrived[step, me] = partial[step, k]

    def own_coefs(step, shifts):
        some = arrived.at[step, pl.ds(0, n - 1)]
        pltpu.make_async_copy(some, some, arrive_sem.at[step]).wait()
        total = jnp.sum(arrived[step], axis=0)
        coefs[step, own] = turn(total, skips[step, own], shifts)

        @pl.loop(1, half)
        def _(by):
            to = lax.rem(own + by, half) * copies + group
            pltpu.make_async_remote_copy(
                src_ref=coefs.at[step, own],
                dst_ref=coefs.at[step, own],
                send_sem=spread_sem.at[step],
                recv_sem=coef_sem.at[step, own],
                device_id={"rows": to},
                device_id_type=MESH,
            ).start()

    has_next, has_last = position < n_pairs - 1, position > 0
    after, before = lax.rem(position + 1, n_pairs), lax.rem(position + n_pairs - 1, n_pairs)

    def lend(k, side, to):
        for at, block in enumerate((k, half + k)):
            pltpu.make_async_remote_copy(
                src_ref=column_block(data, block),
                dst_ref=guests.at[side, at],
                send_sem=guest_sem.at[side, 0],
                recv_sem=guest_sem.at[side, 1],
                device_id={"pairs": to},
                device_id_type=MESH,
            ).start()

    def lend_coefs(k, side, to):
        @pl.loop(0, half)
        def _(at):
            pltpu.make_async_remote_copy(
                src_ref=coefs.at[0, k],
                dst_ref=guest_coefs.at[side],
                send_sem=guest_coef_sem.at[side, 0],
                recv_sem=guest_coef_sem.at[side, 1],
                device_id={"rows": at * copies + group, "pairs": to},
                device_id_type=MESH,
            ).start()

    def wait_bytes(ref, sem):
        pltpu.make_async_copy(ref, ref, sem).wait()

    def wait_guest(side):
        wait_bytes(guests.at[side], guest_sem.at[side, 1])
        wait_bytes(guest_coefs.at[side], guest_coef_sem.at[side, 1])

    def wait_coefs(step, k):
        tile = coefs.at[step, k]

        @pl.when(k != own)
        def _():
            pltpu.make_async_copy(tile, tile, coef_sem.at[step, k]).wait()

    shifts, later = shifts_of(offsets, 0), shifts_of(offsets, 1)

    def first_pair(k):
        upper, lower = column_block(data, k), column_block(data, half + k)
        return upper, lower, turned.at[k], partial.at[0, k]

    def second_pair(k):
        return moved.at[k], moved.at[half + k], turned.at[k], partial.at[1, k]

    early = half // 4

    @pl.loop(0, early)
    def _(at):
        products([first_pair(2 * at), first_pair(2 * at + 1)], shifts, rows)

    pl.semaphore_wait(barrier, n - 1 + (1 + half) * (not_first + 1 - is_last))

    @pl.when(has_next)
    def _():
        lend(half - 1, 0, after)

    @pl.when(has_last)
    def _():
        lend(0, 1, before)


    @pl.loop(0, 2 * early)
    def _(k):
        give(0, k)

    @pl.loop(early, half // 2)
    def _(at):
        products([first_pair(2 * at), first_pair(2 * at + 1)], shifts, rows)
        give(0, 2 * at)
        give(0, 2 * at + 1)

    own_coefs(0, shifts)

    @pl.when(has_next & (own == half - 1))
    def _():
        lend_coefs(half - 1, 0, after)

    @pl.when(has_last & (own == 0))
    def _():
        lend_coefs(0, 1, before)

    def first_turn(k, upper_to, lower_to):
        upper = column_block(data, k)
        return upper, moved.at[upper_to], moved.at[lower_to], coefs.at[0, k], turned.at[k]

    def last_turn(k):
        upper, lower = column_block(rotated, k), column_block(rotated, half + k)
        return moved.at[k], upper, lower, coefs.at[1, k], turned.at[k]

    out_low, out_up = 2 * half, 2 * half + 1
    low_zero = (1 - not_first) + out_low * not_first
    up_last = (2 * half - 1) * is_last + out_up * (1 - is_last)
    def turn_inner(k):
        for each in (k, k + 1):
            wait_coefs(0, each)
        rotate([first_turn(each, each + 1, half + each - 1) for each in (k, k + 1)], shifts[3], rows)

    def multiply(ks):
        products([second_pair(k) for k in ks], later, rows)
        for k in ks:
            give(1, k)

    if half > 2:
        turn_inner(1)

    @pl.loop(1, half // 2 - 1)
    def _(at):
        turn_inner(2 * at + 1)
        multiply((2 * at, 2 * at + 1))

    wait_coefs(0, 0)
    wait_coefs(0, half - 1)
    ends = [first_turn(half - 1, up_last, 2 * half - 2), first_turn(0, not_first, low_zero)]
    rotate(ends, shifts[3], rows)
    if half > 2:
        multiply((1, half - 2))

    @pl.when(position > 0)
    def _():
        wait_guest(0)
        rotate_one(guests.at[0], moved.at[0], guest_coefs.at[0], shifts, rows, 0)

    @pl.when(position < n_pairs - 1)
    def _():
        wait_guest(1)
        rotate_one(guests.at[1], moved.at[2 * half - 1], guest_coefs.at[1], shifts, rows, 1)

    multiply((0, half - 1))
    own_coefs(1, later)

    def turn_last(ks):
        for k in ks:
            wait_coefs(1, k)
        rotate([last_turn(k) for k in ks], later[3], rows)
        for k in ks:
            tile = coefs[1, k] * (1.0 / (rows * n))
            power[pl.ds(k, 1), :] = tile[6:7, :]
            power[pl.ds(half + k, 1), :] = tile[7:8, :]

    @pl.loop(1, half // 2 - 1)
    def _(at):
        turn_last((2 * at, 2 * at + 1))

    if half > 2:
        turn_last((1, half - 2))
    turn_last((0, half - 1))

    for side, lent, lender in ((0, has_next, half - 1), (1, has_last, 0)):

        @pl.when(lent)
        def _():
            wait_bytes(guests.at[side], guest_sem.at[side, 0])

        @pl.when(lent & (own == lender))
        def _():
            wait_bytes(coefs.at[0], guest_coef_sem.at[side, 0])

    for step in range(STEPS):
        some = arrived.at[step, pl.ds(0, n - 1)]
        pltpu.make_async_copy(some, some, give_sem.at[step]).wait()
        rest = coefs.at[step, pl.ds(0, half - 1)]
        pltpu.make_async_copy(rest, rest, spread_sem.at[step]).wait()


def per_device(n, n_pairs, loads, col_weights, partner_offsets, skip_mask):
    rows, columns = loads.shape
    half = columns // (2 * BLOCK)
    tiles = (TILE, BLOCK)
    vmem = pl.BlockSpec(memory_space=pltpu.VMEM)
    smem = pl.BlockSpec(memory_space=pltpu.SMEM)
    dma = pltpu.SemaphoreType.DMA
    weighted = loads * col_weights[None, :]
    rotated, power = pl.pallas_call(
        functools.partial(turning_kernel, n, n_pairs, half, rows),
        out_shape=(
            jax.ShapeDtypeStruct(loads.shape, jnp.float32),
            jax.ShapeDtypeStruct((2 * half, BLOCK), jnp.float32),
        ),
        in_specs=[vmem, smem, smem],
        out_specs=(vmem, vmem),
        scratch_shapes=[
            pltpu.VMEM((2 * half + 2, rows, BLOCK), jnp.float32),
            pltpu.VMEM((STEPS, half) + tiles, jnp.float32),
            pltpu.VMEM((STEPS, n) + tiles, jnp.float32),
            pltpu.VMEM((STEPS, half) + tiles, jnp.float32),
            pltpu.VMEM((half, 3, rows, BLOCK), jnp.float32),
            pltpu.VMEM((2, 2, rows, BLOCK), jnp.float32),
            pltpu.VMEM((2,) + tiles, jnp.float32),
            dma((STEPS,)),
            dma((STEPS,)),
            dma((STEPS,)),
            dma((STEPS, half)),
            dma((2, 2)),
            dma((2, 2)),
        ],
        compiler_params=pltpu.CompilerParams(
            collective_id=0, has_side_effects=True, vmem_limit_bytes=24 * 1024 * 1024
        ),
        cost_estimate=pl.CostEstimate(
            flops=60 * loads.size, bytes_accessed=8 * loads.size, transcendentals=0
        ),
    )(weighted, partner_offsets, skip_mask)
    return rotated, power.reshape(columns)


def solution(mesh):
    in_specs = (P("rows", "pairs"), P("pairs"), P(), P(None, "pairs"))
    out_specs = (P("rows", "pairs"), P("pairs"))
    return jax.shard_map(
        functools.partial(per_device, mesh.shape["rows"], mesh.shape["pairs"]),
        mesh=mesh, in_specs=in_specs, out_specs=out_specs, check_vma=False,
    )
```

```python
import functools
import jax
import jax.numpy as jnp
from jax import lax
from jax.experimental import pallas as pl
from jax.experimental.pallas import tpu as pltpu
from jax.sharding import PartitionSpec as P

BLOCK = 128
STEPS = 2
TILE = 8
CHUNK = 32
DEPTH = 2
MESH = pl.DeviceIdType.MESH


def rolled(x, shift):
    return pltpu.roll(x, shift, 1)


def fold(x):
    return jnp.sum(x.reshape(x.shape[0] // TILE, TILE, BLOCK), axis=0)


def shifts_of(offsets, step):
    first, second = offsets[step, 0], offsets[step, 1]
    to_first = lax.rem(BLOCK - first, BLOCK)
    to_second = lax.rem(BLOCK - second, BLOCK)
    between = lax.rem(BLOCK + first - second, BLOCK)
    return to_first, to_second, between, second


def spots(rows):
    return [pl.ds(at * CHUNK, CHUNK) for at in range(rows // CHUNK)]


class Later:
    def __init__(self):
        self.waiting = []

    def add(self, stores):
        self.waiting.append(stores)
        if len(self.waiting) > DEPTH:
            self.write(self.waiting.pop(0))

    def write(self, stores):
        for ref, index, value in stores:
            ref[index] = value

    def end(self):
        for stores in self.waiting:
            self.write(stores)


def products(pairs, shifts, rows):
    to_first, to_second, between, _ = shifts
    later = Later()
    for upper, lower, turned, partial in pairs:
        sums = [jnp.zeros((TILE, BLOCK), jnp.float32)] * 7
        for spot in spots(rows):
            u, l = upper[spot, :], lower[spot, :]
            lp, ud, ld = rolled(l, to_first), rolled(u, between), rolled(l, to_second)
            factor_pairs = ((u, u), (l, l), (u, lp), (u, ud), (u, ld), (lp, ud), (lp, ld))
            sums = [total + fold(a * b) for total, (a, b) in zip(sums, factor_pairs)]
            later.add([(turned, (at, spot), x) for at, x in enumerate((lp, ud, ld))])
        ends = [jnp.sum(total, axis=0, keepdims=True) for total in sums]
        ends.append(jnp.zeros((1, BLOCK), jnp.float32))
        later.add([(partial, pl.ds(at, 1), x) for at, x in enumerate(ends)])
    later.end()


def angle(a, b, g):
    half_gap = 0.5 * (b - a)
    sign = jnp.where(half_gap >= 0.0, 1.0, -1.0)
    denominator = jnp.maximum(
        jnp.abs(half_gap) + jnp.sqrt(half_gap * half_gap + g * g), 1e-06 * (a + b)
    )
    t = sign * g / denominator
    c = 1.0 / jnp.sqrt(1.0 + t * t)
    return c, t * c


def norms(a, b, g, c, s):
    cross = 2.0 * c * s * g
    return c * c * a - cross + s * s * b, s * s * a + cross + c * c * b


def turn(total, skip, shifts):
    to_first, _, between, back = shifts
    row = [jnp.broadcast_to(total[at : at + 1, :], (TILE, BLOCK)) for at in range(7)]
    a, b, g, u_ud, u_ld, l_ud, l_ld = row
    b = rolled(b, to_first)
    keep = jnp.full((TILE, BLOCK), skip, jnp.int32) == 0
    c, s = angle(a, b, g)
    c, s = jnp.where(keep, c, 1.0), jnp.where(keep, s, 0.0)
    a1, b1 = norms(a, b, g, c, s)
    cd, sd, bd = rolled(c, between), rolled(s, between), rolled(b1, between)
    g1 = c * (sd * u_ud + cd * u_ld) - s * (sd * l_ud + cd * l_ld)
    c2, s2 = angle(a1, bd, g1)
    c2, s2 = jnp.where(keep, c2, 1.0), jnp.where(keep, s2, 0.0)
    a2, b2 = norms(a1, bd, g1, c2, s2)
    place = lax.broadcasted_iota(jnp.int32, (TILE, BLOCK), 0)
    tile = rolled(b2, back)
    for at, value in enumerate((c, s, cd, sd, c2, s2, a2)):
        tile = jnp.where(place == at, value, tile)
    return tile


def factors(coefs):
    tile = coefs[...]
    c, s, cd, sd, c2, s2 = (
        jnp.broadcast_to(tile[at : at + 1, :], (TILE, BLOCK)) for at in range(6)
    )
    up = (c2 * c, -c2 * s, -s2 * sd, -s2 * cd)
    low = (s2 * c, -s2 * s, c2 * sd, c2 * cd)
    return up, low


def mix(weights, parts):
    shape = (CHUNK // TILE, TILE, BLOCK)
    total = sum(w[None] * x.reshape(shape) for w, x in zip(weights, parts))
    return total.reshape(CHUNK, BLOCK)


def rotate(pairs, back, rows):
    later = Later()
    weights = [factors(pair[3]) for pair in pairs]
    for (upper, new_upper, new_lower, _, turned), (up, low) in zip(pairs, weights):
        for spot in spots(rows):
            parts = [upper[spot, :]] + [turned[at, spot, :] for at in range(3)]
            low_part = rolled(mix(low, parts), back)
            later.add([(new_upper, spot, mix(up, parts)), (new_lower, spot, low_part)])
    later.end()


def rotate_one(pair, new, coefs, shifts, rows, which):
    weights = factors(coefs)[which]
    to_first, to_second, between, back = shifts
    later = Later()
    for spot in spots(rows):
        u, l = pair[0, spot, :], pair[1, spot, :]
        parts = (u, rolled(l, to_first), rolled(u, between), rolled(l, to_second))
        x = mix(weights, parts)
        later.add([(new, spot, rolled(x, back) if which else x)])
    later.end()


def each(least, end):
    def run(body):
        for at in range(least, end):
            body(at)

    return run


def column_block(array, block):
    return array.at[:, pl.ds(pl.multiple_of(block * BLOCK, BLOCK), BLOCK)]


def turning_kernel(
    n, n_pairs, half, rows,
    data, offsets, skips,
    rotated, power,
    moved, partial, arrived, coefs, turned, guests, guest_coefs,
    give_sem, arrive_sem, spread_sem, coef_sem, guest_sem, guest_coef_sem,
):
    me, position = lax.axis_index("rows"), lax.axis_index("pairs")
    copies = n // half
    own, group = me // copies, lax.rem(me, copies)
    not_first = (position + n_pairs - 1) // n_pairs
    is_last = (position + 1) // n_pairs

    barrier = pltpu.get_barrier_semaphore()

    @each(1, n)
    def _(by):
        pl.semaphore_signal(
            barrier, inc=1, device_id={"rows": lax.rem(me + by, n)}, device_id_type=MESH
        )

    def greet_pairs(to):
        pl.semaphore_signal(barrier, inc=1, device_id={"pairs": to}, device_id_type=MESH)

        @each(0, half)
        def _(at):
            pl.semaphore_signal(
                barrier, inc=1,
                device_id={"rows": at * copies + group, "pairs": to}, device_id_type=MESH,
            )

    @pl.when(position > 0)
    def _():
        greet_pairs(position - 1)

    @pl.when(position < n_pairs - 1)
    def _():
        greet_pairs(position + 1)

    def give(step, k):
        @each(0, copies)
        def _(at):
            to = k * copies + at

            @pl.when(to != me)
            def _():
                pltpu.make_async_remote_copy(
                    src_ref=partial.at[step, k],
                    dst_ref=arrived.at[step, me],
                    send_sem=give_sem.at[step],
                    recv_sem=arrive_sem.at[step],
                    device_id={"rows": to},
                    device_id_type=MESH,
                ).start()

            @pl.when(to == me)
            def _():
                arrived[step, me] = partial[step, k]

    def own_coefs(step, shifts):
        some = arrived.at[step, pl.ds(0, n - 1)]
        pltpu.make_async_copy(some, some, arrive_sem.at[step]).wait()
        total = jnp.sum(arrived[step], axis=0)
        coefs[step, own] = turn(total, skips[step, own], shifts)

        @each(1, half)
        def _(by):
            to = lax.rem(own + by, half) * copies + group
            pltpu.make_async_remote_copy(
                src_ref=coefs.at[step, own],
                dst_ref=coefs.at[step, own],
                send_sem=spread_sem.at[step],
                recv_sem=coef_sem.at[step, own],
                device_id={"rows": to},
                device_id_type=MESH,
            ).start()

    has_next, has_last = position < n_pairs - 1, position > 0
    after, before = lax.rem(position + 1, n_pairs), lax.rem(position + n_pairs - 1, n_pairs)

    def lend(k, side, to):
        for at, block in enumerate((k, half + k)):
            pltpu.make_async_remote_copy(
                src_ref=column_block(data, block),
                dst_ref=guests.at[side, at],
                send_sem=guest_sem.at[side, 0],
                recv_sem=guest_sem.at[side, 1],
                device_id={"pairs": to},
                device_id_type=MESH,
            ).start()

    def lend_coefs(k, side, to):
        @each(0, half)
        def _(at):
            pltpu.make_async_remote_copy(
                src_ref=coefs.at[0, k],
                dst_ref=guest_coefs.at[side],
                send_sem=guest_coef_sem.at[side, 0],
                recv_sem=guest_coef_sem.at[side, 1],
                device_id={"rows": at * copies + group, "pairs": to},
                device_id_type=MESH,
            ).start()

    def wait_bytes(ref, sem):
        pltpu.make_async_copy(ref, ref, sem).wait()

    def wait_guest(side):
        wait_bytes(guests.at[side], guest_sem.at[side, 1])
        wait_bytes(guest_coefs.at[side], guest_coef_sem.at[side, 1])

    def wait_coefs(step, k):
        tile = coefs.at[step, k]

        @pl.when(k != own)
        def _():
            pltpu.make_async_copy(tile, tile, coef_sem.at[step, k]).wait()

    shifts, later = shifts_of(offsets, 0), shifts_of(offsets, 1)

    def first_pair(k):
        upper, lower = column_block(data, k), column_block(data, half + k)
        return upper, lower, turned.at[k], partial.at[0, k]

    def second_pair(k):
        return moved.at[k], moved.at[half + k], turned.at[k], partial.at[1, k]

    early = half // 4

    @pl.loop(0, early)
    def _(at):
        products([first_pair(2 * at), first_pair(2 * at + 1)], shifts, rows)

    pl.semaphore_wait(barrier, n - 1 + (1 + half) * (not_first + 1 - is_last))

    @pl.when(has_next)
    def _():
        lend(half - 1, 0, after)

    @pl.when(has_last)
    def _():
        lend(0, 1, before)


    @pl.loop(0, 2 * early)
    def _(k):
        give(0, k)

    @pl.loop(early, half // 2)
    def _(at):
        products([first_pair(2 * at), first_pair(2 * at + 1)], shifts, rows)
        give(0, 2 * at)
        give(0, 2 * at + 1)

    own_coefs(0, shifts)

    @pl.when(has_next & (own == half - 1))
    def _():
        lend_coefs(half - 1, 0, after)

    @pl.when(has_last & (own == 0))
    def _():
        lend_coefs(0, 1, before)

    def first_turn(k, upper_to, lower_to):
        upper = column_block(data, k)
        return upper, moved.at[upper_to], moved.at[lower_to], coefs.at[0, k], turned.at[k]

    def last_turn(k):
        upper, lower = column_block(rotated, k), column_block(rotated, half + k)
        return moved.at[k], upper, lower, coefs.at[1, k], turned.at[k]

    out_low, out_up = 2 * half, 2 * half + 1
    low_zero = (1 - not_first) + out_low * not_first
    up_last = (2 * half - 1) * is_last + out_up * (1 - is_last)
    def turn_inner(k):
        for each in (k, k + 1):
            wait_coefs(0, each)
        rotate([first_turn(each, each + 1, half + each - 1) for each in (k, k + 1)], shifts[3], rows)

    def multiply(ks):
        products([second_pair(k) for k in ks], later, rows)
        for k in ks:
            give(1, k)

    if half > 2:
        turn_inner(1)

    @pl.loop(1, half // 2 - 1)
    def _(at):
        turn_inner(2 * at + 1)
        multiply((2 * at, 2 * at + 1))

    wait_coefs(0, 0)
    wait_coefs(0, half - 1)
    ends = [first_turn(half - 1, up_last, 2 * half - 2), first_turn(0, not_first, low_zero)]
    rotate(ends, shifts[3], rows)
    if half > 2:
        multiply((1, half - 2))

    @pl.when(position > 0)
    def _():
        wait_guest(0)
        rotate_one(guests.at[0], moved.at[0], guest_coefs.at[0], shifts, rows, 0)

    @pl.when(position < n_pairs - 1)
    def _():
        wait_guest(1)
        rotate_one(guests.at[1], moved.at[2 * half - 1], guest_coefs.at[1], shifts, rows, 1)

    multiply((0, half - 1))
    own_coefs(1, later)

    def turn_last(ks):
        for k in ks:
            wait_coefs(1, k)
        rotate([last_turn(k) for k in ks], later[3], rows)
        for k in ks:
            tile = coefs[1, k] * (1.0 / (rows * n))
            power[pl.ds(k, 1), :] = tile[6:7, :]
            power[pl.ds(half + k, 1), :] = tile[7:8, :]

    @pl.loop(1, half // 2 - 1)
    def _(at):
        turn_last((2 * at, 2 * at + 1))

    if half > 2:
        turn_last((1, half - 2))
    turn_last((0, half - 1))

    for side, lent, lender in ((0, has_next, half - 1), (1, has_last, 0)):

        @pl.when(lent)
        def _():
            wait_bytes(guests.at[side], guest_sem.at[side, 0])

        @pl.when(lent & (own == lender))
        def _():
            wait_bytes(coefs.at[0], guest_coef_sem.at[side, 0])

    for step in range(STEPS):
        some = arrived.at[step, pl.ds(0, n - 1)]
        pltpu.make_async_copy(some, some, give_sem.at[step]).wait()
        rest = coefs.at[step, pl.ds(0, half - 1)]
        pltpu.make_async_copy(rest, rest, spread_sem.at[step]).wait()


def per_device(n, n_pairs, loads, col_weights, partner_offsets, skip_mask):
    rows, columns = loads.shape
    half = columns // (2 * BLOCK)
    tiles = (TILE, BLOCK)
    vmem = pl.BlockSpec(memory_space=pltpu.VMEM)
    smem = pl.BlockSpec(memory_space=pltpu.SMEM)
    dma = pltpu.SemaphoreType.DMA
    weighted = loads * col_weights[None, :]
    rotated, power = pl.pallas_call(
        functools.partial(turning_kernel, n, n_pairs, half, rows),
        out_shape=(
            jax.ShapeDtypeStruct(loads.shape, jnp.float32),
            jax.ShapeDtypeStruct((2 * half, BLOCK), jnp.float32),
        ),
        in_specs=[vmem, smem, smem],
        out_specs=(vmem, vmem),
        scratch_shapes=[
            pltpu.VMEM((2 * half + 2, rows, BLOCK), jnp.float32),
            pltpu.VMEM((STEPS, half) + tiles, jnp.float32),
            pltpu.VMEM((STEPS, n) + tiles, jnp.float32),
            pltpu.VMEM((STEPS, half) + tiles, jnp.float32),
            pltpu.VMEM((half, 3, rows, BLOCK), jnp.float32),
            pltpu.VMEM((2, 2, rows, BLOCK), jnp.float32),
            pltpu.VMEM((2,) + tiles, jnp.float32),
            dma((STEPS,)),
            dma((STEPS,)),
            dma((STEPS,)),
            dma((STEPS, half)),
            dma((2, 2)),
            dma((2, 2)),
        ],
        compiler_params=pltpu.CompilerParams(
            collective_id=0, has_side_effects=True, vmem_limit_bytes=24 * 1024 * 1024
        ),
        cost_estimate=pl.CostEstimate(
            flops=60 * loads.size, bytes_accessed=8 * loads.size, transcendentals=0
        ),
    )(weighted, partner_offsets, skip_mask)
    return rotated, power.reshape(columns)


def solution(mesh):
    in_specs = (P("rows", "pairs"), P("pairs"), P(), P(None, "pairs"))
    out_specs = (P("rows", "pairs"), P("pairs"))
    return jax.shard_map(
        functools.partial(per_device, mesh.shape["rows"], mesh.shape["pairs"]),
        mesh=mesh, in_specs=in_specs, out_specs=out_specs, check_vma=False,
    )
```
